256 devices in a mesh: dp: 16 (over z, x_hi), ctx: 16 (over y, x_lo, core).
Axes of the slice: x: 4 (x_hi: 2, x_lo: 2; x = x_hi * 2 + x_lo), y: 4, z: 8, core: 2. Of those that a mesh axis runs over, the one named last changes fastest.
Arguments:
- query_rows: bfloat16 [16, 3584, 1024], P('dp', 'ctx'), may hold values from -48 to 48
- key_rows: bfloat16 [16, 3584, 128], P('dp', 'ctx'), may hold values from -4 to 4
- value_rows: bfloat16 [16, 3584, 128], P('dp', 'ctx'), may hold values from -5 to 5
- out_grad: bfloat16 [16, 3584, 1024], P('dp', 'ctx'), may hold values from -5 to 5
- doc_ids: int32 [16, 3584], P('dp'), may hold values from 0 to 7, never falling along the last dimension, each value on 1 to 2688 neighbouring positions
- matching: int32 [16], replicated, may hold values from 0 to 15, as said below
Outputs:
- attended: bfloat16 [16, 3584, 1024], P('dp', 'ctx')
- query_grad: bfloat16 [16, 3584, 1024], P('dp', 'ctx')
- key_grad: bfloat16 [16, 3584, 128], P('dp', 'ctx')
- value_grad: bfloat16 [16, 3584, 128], P('dp', 'ctx')
The draws below stay inside these ranges and needn't reach their ends.
Inputs may be any that keep to these rules, and one draw needn't show every extreme that they name: matching[b] is b XOR m for one m of 1 to 15 shared by all b, so micro-batches come in pairs.
All inputs are finite; a program needn't handle non-finite values.
Results may differ from the reference program's by a relative error of at most 0.035.
Values may be sent and summed in bfloat16 or wider, within the bound.
No kernel may reach another device: no remote copies, remote signals or barrier semaphores. Data moves between devices by JAX's collectives and lax.ppermute only.
A program may use at most 64 MiB of HBM per device.

```python
import math
import jax
import jax.numpy as jnp
import numpy as np
from jax import lax

H = 8
DH = 128
SPAN = 224
DOCS = 8
SEQ = 3584
N_DP = 16


def query_key_pair(key):
    query_shape = (N_DP, SEQ, H * DH)
    key_shape = (N_DP, SEQ, DH)
    keys_out = jax.random.truncated_normal(jax.random.fold_in(key, 11), -4.0, 4.0, key_shape, jnp.float32)
    queries_out = 2.0 * jax.random.truncated_normal(jax.random.fold_in(key, 12), -4.0, 4.0, query_shape, jnp.float32)
    return (queries_out, keys_out)


def draw_query_rows(key, part):
    return query_key_pair(key)[0].astype(jnp.bfloat16)


def draw_key_rows(key, part):
    return query_key_pair(key)[1].astype(jnp.bfloat16)


def draw_matching(key, part):
    key = jax.random.fold_in(key, 53)
    choices_list = jax.random.permutation(key, jnp.arange(1, N_DP, dtype=jnp.int32))
    flip_mask = choices_list[0].astype(jnp.int32)
    return jnp.bitwise_xor(jnp.arange(N_DP, dtype=jnp.int32), flip_mask).astype(jnp.int32)


def block_levels(own_key, extent, split, least, largest):
    factor_of = 1.0
    for axis_at, parts in split:
        steps = jax.random.uniform(jax.random.fold_in(jax.random.fold_in(own_key, 6), axis_at), (parts,), jnp.float32, least / len(split), largest / len(split))
        factor_of = factor_of * jnp.repeat(jnp.exp(steps), extent[axis_at] // parts).reshape((-1,) + (1,) * (len(extent) - 1 - axis_at))
    return factor_of


def split_up(count, total, bound, slope):
    loads = [(1 << 20) // math.isqrt(rank ** slope) + 1 for rank in range(2, count + 1)]
    spare, holding = total - bound - (count - 1), [1] * (count - 1)
    while spare > 0:
        movable = [i for i in range(count - 1) if holding[i] < bound]
        pool, budget = sum([loads[i] for i in movable]), spare
        for i in movable:
            extra = min(bound - holding[i], max(1, budget * loads[i] // pool), spare)
            holding[i] = holding[i] + extra
            spare = spare - extra
    return np.array([bound] + holding)


def ragged(stream_key, number_of, total, limit, skew):
    if number_of == 2:
        one = jax.random.randint(stream_key, (), max(1, total - limit), min(limit, total - 1) + 1)
        return jnp.stack([one, total - one])
    lengths = jnp.asarray(split_up(number_of, total, limit, skew), jnp.int32)
    twos = (number_of - 1) // 2
    donor, receiver = lengths[1:1 + 2 * twos:2], lengths[2:2 + 2 * twos:2]
    room = jnp.minimum(donor - 1, limit - receiver)
    shifted = jax.random.randint(jax.random.fold_in(stream_key, 1), (twos,), 0, 1 << 20) % (room + 1)
    lengths = lengths.at[1:1 + 2 * twos:2].set(donor - shifted).at[2:2 + 2 * twos:2].set(receiver + shifted)
    return lengths[jax.random.permutation(jax.random.fold_in(stream_key, 2), number_of)]


def gaussian(stream_key, dims, spread, most, pieces=(), held_as=jnp.bfloat16):
    loudness = block_levels(stream_key, dims, pieces, -0.22, 0.18) if pieces else 1.0
    entries = jax.random.normal(stream_key, dims, jnp.float32) * spread * loudness
    return jnp.minimum(jnp.maximum(entries, -most), most).astype(held_as)


def setup_inputs(seed: int = 0) -> dict:
    key_list = jax.random.split(jax.random.key(seed), 7)
    query_rows = draw_query_rows(jax.random.fold_in(key_list[6], 71), 0)
    key_rows = draw_key_rows(jax.random.fold_in(key_list[6], 71), 0)
    value_rows = gaussian(key_list[2], (N_DP, SEQ, DH), 1.0, 5.0, ((0, 16), (1, 16)))
    out_grad = gaussian(key_list[3], (N_DP, SEQ, H * DH), 1.0, 5.0, ((0, 16), (1, 16)))
    doc_ids = jax.vmap(lambda own: jnp.searchsorted(jnp.cumsum(ragged(own, DOCS, SEQ, 3 * SEQ // 4, 2)), jnp.arange(SEQ), side="right"))(jax.random.split(key_list[4], N_DP)).reshape((N_DP, SEQ)).astype(jnp.int32)
    matching = draw_matching(jax.random.fold_in(key_list[6], 71), 0)
    return dict(query_rows=query_rows, key_rows=key_rows, value_rows=value_rows, out_grad=out_grad, doc_ids=doc_ids, matching=matching)


def reorder(stacked, matching):
    head_part = stacked[:, :SEQ - SPAN]
    tail_part = jnp.take(stacked[:, SEQ - SPAN:], matching, axis=0)
    return jnp.concatenate([head_part, tail_part], axis=1)

def one_batch(inputs):
    query_two, key_two, value_two, grad_two, doc_row = inputs
    seq_len = query_two.shape[0]
    head_width = key_two.shape[1]
    head_count = query_two.shape[1] // head_width
    score_scale = 1.0 / math.sqrt(head_width)
    query_heads = query_two.reshape(seq_len, head_count, head_width).transpose(1, 0, 2).astype(jnp.float32)
    grad_heads = grad_two.reshape(seq_len, head_count, head_width).transpose(1, 0, 2).astype(jnp.float32)
    key_wide = key_two.astype(jnp.float32)
    value_wide = value_two.astype(jnp.float32)
    places = jnp.arange(seq_len, dtype=jnp.int32)
    allowed = (places[None, :] <= places[:, None]) & (doc_row[None, :] == doc_row[:, None])
    scores = jnp.einsum('hcd,kd->hck', query_heads, key_wide) * score_scale
    scores = jnp.where(allowed[None], scores, -jnp.inf)
    row_top = lax.optimization_barrier(jnp.max(scores, axis=-1, keepdims=True))
    log_total = row_top + jnp.log(lax.optimization_barrier(jnp.sum(jnp.exp(scores - row_top), axis=-1, keepdims=True)))
    probs = jnp.exp(scores - log_total)
    weights = probs.astype(jnp.bfloat16)
    out_heads = jnp.einsum('hck,kd->hcd', weights.astype(jnp.float32), value_wide).astype(jnp.bfloat16)
    row_dot = lax.optimization_barrier(jnp.sum(grad_heads * out_heads.astype(jnp.float32), axis=-1, keepdims=True))
    dprob = jnp.einsum('hcd,kd->hck', grad_heads, value_wide)
    dscore = (probs * (dprob - row_dot)).astype(jnp.bfloat16)
    dscore_wide = dscore.astype(jnp.float32)
    query_grad = (score_scale * jnp.einsum('hck,kd->hcd', dscore_wide, key_wide)).astype(jnp.bfloat16)
    key_grad = (score_scale * jnp.einsum('hck,hcd->kd', dscore_wide, query_heads)).astype(jnp.bfloat16)
    value_grad = jnp.einsum('hck,hcd->kd', weights.astype(jnp.float32), grad_heads).astype(jnp.bfloat16)
    attended = out_heads.transpose(1, 0, 2).reshape(seq_len, head_count * head_width)
    query_grad = query_grad.transpose(1, 0, 2).reshape(seq_len, head_count * head_width)
    return (attended, query_grad, key_grad, value_grad)

def reference(query_rows, key_rows, value_rows, out_grad, doc_ids, matching):
    arranged = (reorder(query_rows, matching), reorder(key_rows, matching), reorder(value_rows, matching), reorder(out_grad, matching), doc_ids)
    attended, query_grad, key_grad, value_grad = lax.map(one_batch, arranged)
    return (reorder(attended, matching), reorder(query_grad, matching), reorder(key_grad, matching), reorder(value_grad, matching))
```

```python
import functools
import math

import jax
import jax.numpy as jnp
from jax import lax
from jax.experimental import pallas as pl
from jax.experimental.pallas import tpu as pltpu
from jax.sharding import PartitionSpec as P

TILE = 256
LANES = 256


def dot(a, b, ca, cb):
    return lax.dot_general(a, b, (((ca,), (cb,)), ((), ())), preferred_element_type=jnp.float32)


def attention_kernel(
    heads, width, span, scale,
    bounds, low, query, grad, pairs,
    out, dquery, dpairs,
    q_rows, g_cols, scores, weights, dscores, out_t, dq_t, top, total,
):
    rows = heads * span
    tiles = pairs.shape[0] // TILE
    chunks = [slice(r, r + LANES) for r in range(0, rows, LANES)]
    first, clear, full, last, offset = (bounds[i] for i in range(5))
    factor = scale * math.log2(math.e)

    for h in range(heads):
        q_rows[h * span : (h + 1) * span, :] = query[:, h * width : (h + 1) * width]
        g_cols_rows = grad[:, h * width : (h + 1) * width]
        dscores[h * span : (h + 1) * span, 0:width] = g_cols_rows
    top[...] = jnp.full(top.shape, -jnp.inf, jnp.float32)
    total[...] = jnp.zeros(total.shape, jnp.float32)
    out_t[...] = jnp.zeros(out_t.shape, jnp.float32)
    dq_t[...] = jnp.zeros(dq_t.shape, jnp.float32)

    def keys_at(t):
        return pl.ds(pl.multiple_of(t * TILE, TILE), TILE)

    def score_tile(t, masked):
        at = keys_at(t)
        key = pairs[at, 0:width]
        for c in chunks:
            s = dot(key, q_rows[c, :], 1, 1)
            if masked:
                place = t * TILE + lax.broadcasted_iota(jnp.int32, (TILE, LANES), 0)
                ok = (place >= low[0:1, c]) & (place <= low[1:2, c])
                s = jnp.where(ok, s, -jnp.inf)
            scores[at, c] = s
            top[:, c] = jnp.maximum(top[:, c], jnp.max(s.reshape(TILE // 8, 8, LANES), axis=0))

    @pl.loop(first, clear)
    def _(t):
        score_tile(t, True)

    @pl.loop(clear, full)
    def _(t):
        score_tile(t, False)

    @pl.loop(full, last)
    def _(t):
        score_tile(t, True)

    peak = jnp.max(top[...], axis=0, keepdims=True) * factor
    top[...] = jnp.broadcast_to(peak, top.shape)

    @pl.loop(first, last)
    def _(t):
        at = keys_at(t)
        value_t = pairs[at, width : 2 * width].T
        for c in chunks:
            p = jnp.exp2(scores[at, c] * factor - top[0:1, c])
            total[:, c] += jnp.sum(p.reshape(TILE // 8, 8, LANES), axis=0)
            pb = p.astype(jnp.bfloat16)
            weights[at, c] = pb
            out_t[:, c] += dot(value_t, pb, 1, 0)

    inverse = 1.0 / jnp.sum(total[...], axis=0, keepdims=True)
    for r in range(0, rows, 128):
        c = slice(r, r + 128)
        o = out_t[:, c] * inverse[:, c]
        g = (dscores[c, 0:width].T.astype(jnp.float32) * inverse[:, c]).astype(jnp.bfloat16)
        g_cols[:, c] = g
        top[0:1, c] = jnp.sum(g.astype(jnp.float32) * o, axis=0, keepdims=True)
        q_at = o.T.astype(jnp.bfloat16)
        weights_out(out, q_at, r, span, width)

    for t in range(tiles):
        @pl.when((t < first) | (t >= last))
        def _():
            dpairs[t * TILE : (t + 1) * TILE, :] = jnp.zeros((TILE, 2 * width), jnp.bfloat16)

    @pl.loop(first, last)
    def _(t):
        at = keys_at(t)
        key = pairs[at, 0:width]
        key_t = key.T
        value = pairs[at, width : 2 * width]
        for c in chunks:
            dp = dot(value, g_cols[:, c], 1, 0)
            ds = weights[at, c] * (dp - top[0:1, c]).astype(jnp.bfloat16)
            dscores[0:TILE, c] = ds
            dq_t[:, c] += dot(key_t, ds, 1, 0)
        dk = dot(dscores[0:TILE, :], q_rows[...], 1, 0)
        dv = dot(weights[at, :], g_cols[...], 1, 1)
        dpairs[at, 0:width] = (dk * scale).astype(jnp.bfloat16)
        dpairs[at, width : 2 * width] = dv.astype(jnp.bfloat16)

    for r in range(0, rows, 128):
        d = (dq_t[:, r : r + 128].T * scale).astype(jnp.bfloat16)
        weights_out(dquery, d, r, span, width)


def weights_out(ref, block, start, span, width):
    done = 0
    while done < block.shape[0]:
        h, at = divmod(start + done, span)
        n = min(block.shape[0] - done, span - at)
        ref[at : at + n, h * width : (h + 1) * width] = block[done : done + n, :]
        done += n


def attention(bounds, low, query, grad, pairs, width):
    span, features = query.shape
    heads = features // width
    rows, keys = heads * span, pairs.shape[0]
    kernel = functools.partial(attention_kernel, heads, width, span, 1.0 / math.sqrt(width))
    vmem = pl.BlockSpec(memory_space=pltpu.VMEM)
    return pl.pallas_call(
        kernel,
        out_shape=(
            jax.ShapeDtypeStruct((span, features), jnp.bfloat16),
            jax.ShapeDtypeStruct((span, features), jnp.bfloat16),
            jax.ShapeDtypeStruct((keys, 2 * width), jnp.bfloat16),
        ),
        in_specs=[pl.BlockSpec(memory_space=pltpu.SMEM), vmem, vmem, vmem, vmem],
        out_specs=(vmem, vmem, vmem),
        scratch_shapes=[
            pltpu.VMEM((rows, width), jnp.bfloat16),
            pltpu.VMEM((width, rows), jnp.bfloat16),
            pltpu.VMEM((keys, rows), jnp.float32),
            pltpu.VMEM((keys, rows), jnp.bfloat16),
            pltpu.VMEM((rows, rows), jnp.bfloat16),
            pltpu.VMEM((width, rows), jnp.float32),
            pltpu.VMEM((width, rows), jnp.float32),
            pltpu.VMEM((8, rows), jnp.float32),
            pltpu.VMEM((8, rows), jnp.float32),
        ],
        compiler_params=pltpu.CompilerParams(vmem_limit_bytes=58 * 1024 * 1024),
        cost_estimate=pl.CostEstimate(
            flops=12 * rows * keys * width // 2, bytes_accessed=6 << 20, transcendentals=rows * keys // 2
        ),
        name="attention",
    )(bounds, low, query, grad, pairs)


def across(block, matching, dp_size):
    def turn(mask):
        return lambda v: lax.ppermute(v, "dp", [(i, i ^ mask) for i in range(dp_size)])

    return lax.switch(matching[0] - 1, [turn(mask) for mask in range(1, dp_size)], block)


def on_device(query_rows, key_rows, value_rows, out_grad, doc_ids, matching):
    ctx_size = lax.axis_size("ctx")
    dp_size = lax.axis_size("dp")
    me = lax.axis_index("ctx")
    span = query_rows.shape[1]
    width = key_rows.shape[2]
    heads = query_rows.shape[2] // width
    is_last = me == ctx_size - 1
    docs = doc_ids[0]
    offset = me * span

    docs_count = 8
    names = jnp.arange(docs_count, dtype=jnp.int32)[:, None]
    starts = jnp.sum((docs[None, :] < names).astype(jnp.int32), axis=1, keepdims=True)

    def low_of(part):
        return jnp.sum(jnp.where(part[None, :] == names, starts, 0), axis=0)

    low_mine = low_of(lax.dynamic_slice_in_dim(docs, offset, span))
    low_tail = low_of(docs[-span:])
    stored = jnp.concatenate([key_rows[0], value_rows[0]], axis=1)
    extra = jnp.stack([low_tail // 64, low_tail % 64]).astype(jnp.bfloat16)
    extra = jnp.pad(extra, ((0, 14), (0, 2 * width - span)))
    arrived = across(jnp.concatenate([stored, extra], axis=0), matching, dp_size)
    low_sent = arrived[span : span + 2, :span].astype(jnp.int32)
    low = jnp.where(is_last, low_sent[0] * 64 + low_sent[1], low_mine)
    to_last = jnp.where(is_last, stored, arrived[:span])
    sending = jnp.concatenate(
        [jnp.broadcast_to(stored[None], (ctx_size - 1,) + stored.shape), to_last[None]], axis=0
    )
    pairs = lax.all_to_all(sending, "ctx", 0, 0).reshape(ctx_size * span, 2 * width)

    end = offset + span
    first = low[0] // TILE
    last = (end + TILE - 1) // TILE
    clear = jnp.minimum((low[span - 1] + TILE - 1) // TILE, last)
    full = jnp.maximum((offset + 1) // TILE, clear)
    bounds = jnp.stack([first, clear, full, last, offset]).astype(jnp.int32)
    place = offset + jnp.arange(span, dtype=jnp.int32)
    limits = jnp.tile(jnp.stack([low, place]), (1, heads))

    out, dquery, dpairs = attention(bounds, limits, query_rows[0], out_grad[0], pairs, width)
    terms = lax.all_to_all(dpairs.reshape(ctx_size, span, 2 * width), "ctx", 0, 0)
    own = jnp.sum(terms[: ctx_size - 1].astype(jnp.float32), axis=0)
    tail = terms[ctx_size - 1]
    back = across(tail, matching, dp_size)
    final = jnp.where(
        is_last, tail.astype(jnp.float32), own + back.astype(jnp.float32)
    ).astype(jnp.bfloat16)
    return out[None], dquery[None], final[None, :, :width], final[None, :, width:]


def solution(mesh):
    rows = P("dp", "ctx", None)
    return jax.shard_map(
        on_device,
        mesh=mesh,
        in_specs=(rows, rows, rows, rows, P("dp", None), P()),
        out_specs=(rows, rows, rows, rows),
        check_vma=False,
    )
```

```python
import functools
import math

import jax
import jax.numpy as jnp
from jax import lax
from jax.experimental import pallas as pl
from jax.experimental.pallas import tpu as pltpu
from jax.sharding import PartitionSpec as P

TILE = 512
LANES = 256


def dot(a, b, ca, cb):
    return lax.dot_general(a, b, (((ca,), (cb,)), ((), ())), preferred_element_type=jnp.float32)


def attention_kernel(
    heads, width, span, scale,
    bounds, low, query, grad, tail, mine, other,
    out, dquery, same, cross,
    q_rows, g_rows, o_rows, g_cols, pairs, dpairs, scores, weights, dscores, out_t, dq_t, top, total,
    in_sem, pair_sem, out_sem,
):
    rows = heads * span
    keys = pairs.shape[0]
    groups = mine.shape[0]
    features = heads * width
    chunks = [slice(r, r + LANES) for r in range(0, rows, LANES)]
    base, count, clear, full, core, is_last = (bounds[i] for i in range(6))
    factor = scale * math.log2(math.e)

    def head_copies(wide, stacked, sem, to_stacked):
        made = []
        for h in range(heads):
            a = wide.at[:, h * width : (h + 1) * width]
            b = stacked.at[h * span : (h + 1) * span, :]
            a, b = (a, b) if to_stacked else (b, a)
            made.append(pltpu.make_async_copy(a, b, sem.at[h]))
        return made

    def block_rows(k, parity):
        return pl.ds(pl.multiple_of((2 * k + parity) * span, 32), span)

    own_q = head_copies(query, q_rows, in_sem.at[0], True)
    own_g = head_copies(grad, g_rows, in_sem.at[1], True)
    far_q = head_copies(tail.at[:, 0:features], q_rows, in_sem.at[0], True)
    far_g = head_copies(tail.at[:, features : 2 * features], g_rows, in_sem.at[1], True)
    far_pair = pltpu.make_async_copy(
        tail.at[:, 2 * features : 2 * features + 2 * width], pairs.at[keys - span : keys, :], pair_sem.at[0, groups - 1]
    )
    pair_in, pair_out = [], []
    for side, parity in enumerate((core, 1 - core)):
        for k in range(groups):
            at, sem = block_rows(k, parity), pair_sem.at[side, k]
            pair_in.append(pltpu.make_async_copy((mine, other)[side].at[k], pairs.at[at], sem))
            pair_out.append(pltpu.make_async_copy(dpairs.at[at], (same, cross)[side].at[k], sem))
    at_end = is_last == 1

    @pl.when(at_end)
    def _():
        for c in far_q + far_g:
            c.start()
        far_pair.start()

    @pl.when(jnp.logical_not(at_end))
    def _():
        for c in own_q + own_g:
            c.start()
        pair_in[groups - 1].start()

    for i, c in enumerate(pair_in):
        if i != groups - 1:
            c.start()

    top[...] = jnp.full(top.shape, -jnp.inf, jnp.float32)
    total[...] = jnp.zeros(total.shape, jnp.float32)
    out_t[...] = jnp.zeros(out_t.shape, jnp.float32)
    dq_t[...] = jnp.zeros(dq_t.shape, jnp.float32)
    dpairs[...] = jnp.zeros(dpairs.shape, jnp.bfloat16)
    for c in own_q:
        c.wait()
    for c in pair_in:
        c.wait()

    def keys_at(t):
        return pl.ds(pl.multiple_of(base + t * TILE, 32), TILE)

    def kept_at(t):
        return pl.ds(pl.multiple_of(t * TILE, TILE), TILE)

    def score_tile(t, masked):
        key = pairs[keys_at(t), 0:width]
        for c in chunks:
            s = dot(key, q_rows[c, :], 1, 1)
            if masked:
                place = base + t * TILE + lax.broadcasted_iota(jnp.int32, (TILE, LANES), 0)
                ok = (place >= low[0:1, c]) & (place <= low[1:2, c])
                s = jnp.where(ok, s, -jnp.inf)
            scores[kept_at(t), c] = s
            top[:, c] = jnp.maximum(top[:, c], jnp.max(s.reshape(TILE // 8, 8, LANES), axis=0))

    @pl.loop(0, clear)
    def _(t):
        score_tile(t, True)

    @pl.loop(clear, full)
    def _(t):
        score_tile(t, False)

    @pl.loop(full, count)
    def _(t):
        score_tile(t, True)

    peak = jnp.max(top[...], axis=0, keepdims=True) * factor
    top[...] = jnp.broadcast_to(peak, top.shape)

    @pl.loop(0, count)
    def _(t):
        value_t = pairs[keys_at(t), width : 2 * width].T
        for c in chunks:
            p = jnp.exp2(scores[kept_at(t), c] * factor - top[0:1, c])
            total[:, c] += jnp.sum(p.reshape(TILE // 8, 8, LANES), axis=0)
            weights[kept_at(t), c] = p.astype(jnp.bfloat16)
        out_t[...] += dot(value_t, weights[kept_at(t), :], 1, 0)

    for c in own_g:
        c.wait()
    inverse = 1.0 / jnp.sum(total[...], axis=0, keepdims=True)
    for r in range(0, rows, 128):
        c = slice(r, r + 128)
        o = out_t[:, c] * inverse[:, c]
        g = (g_rows[c, :].T.astype(jnp.float32) * inverse[:, c]).astype(jnp.bfloat16)
        g_cols[:, c] = g
        top[0:1, c] = jnp.sum(g.astype(jnp.float32) * o, axis=0, keepdims=True)
        o_rows[c, :] = o.T.astype(jnp.bfloat16)
    out_copies = head_copies(out, o_rows, out_sem.at[0], False)
    for c in out_copies:
        c.start()

    @pl.loop(0, count)
    def _(t):
        at = keys_at(t)
        kept = kept_at(t)
        key = pairs[at, 0:width]
        key_t = key.T
        value = pairs[at, width : 2 * width]
        dv = dot(weights[kept, :], g_cols[...], 1, 1)
        dpairs[at, width : 2 * width] = dv.astype(jnp.bfloat16)
        for c in chunks:
            dp = dot(value, g_cols[:, c], 1, 0)
            dscores[:, c] = weights[kept, c] * (dp - top[0:1, c]).astype(jnp.bfloat16)
        dk = dot(dscores[...], q_rows[...], 1, 0)
        dpairs[at, 0:width] = (dk * scale).astype(jnp.bfloat16)
        dq_t[...] += dot(key_t, dscores[...], 1, 0)

    for c in pair_out:
        c.start()
    for r in range(0, rows, 128):
        g_rows[r : r + 128, :] = (dq_t[:, r : r + 128].T * scale).astype(jnp.bfloat16)
    last_copies = head_copies(dquery, g_rows, out_sem.at[1], False)
    for c in last_copies:
        c.start()
    for c in out_copies + pair_out + last_copies:
        c.wait()


def attention(bounds, low, query, grad, tail, mine, other, width):
    span, features = query.shape
    heads = features // width
    groups = mine.shape[0]
    rows, keys = heads * span, 2 * groups * span
    kernel = functools.partial(attention_kernel, heads, width, span, 1.0 / math.sqrt(width))
    vmem, hbm = pl.BlockSpec(memory_space=pltpu.VMEM), pl.BlockSpec(memory_space=pl.ANY)
    bf16, f32 = jnp.bfloat16, jnp.float32
    return pl.pallas_call(
        kernel,
        out_shape=(
            jax.ShapeDtypeStruct((span, features), bf16),
            jax.ShapeDtypeStruct((span, features), bf16),
            jax.ShapeDtypeStruct(mine.shape, bf16),
            jax.ShapeDtypeStruct(mine.shape, bf16),
        ),
        in_specs=[pl.BlockSpec(memory_space=pltpu.SMEM), vmem] + [hbm] * 5,
        out_specs=(hbm,) * 4,
        scratch_shapes=[
            pltpu.VMEM((rows, width), bf16),
            pltpu.VMEM((rows, width), bf16),
            pltpu.VMEM((rows, width), bf16),
            pltpu.VMEM((width, rows), bf16),
            pltpu.VMEM((keys, 2 * width), bf16),
            pltpu.VMEM((keys, 2 * width), bf16),
            pltpu.VMEM((keys, rows), f32),
            pltpu.VMEM((keys, rows), bf16),
            pltpu.VMEM((TILE, rows), bf16),
            pltpu.VMEM((width, rows), f32),
            pltpu.VMEM((width, rows), f32),
            pltpu.VMEM((8, rows), f32),
            pltpu.VMEM((8, rows), f32),
            pltpu.SemaphoreType.DMA((2, heads)),
            pltpu.SemaphoreType.DMA((2, groups)),
            pltpu.SemaphoreType.DMA((2, heads)),
        ],
        compiler_params=pltpu.CompilerParams(vmem_limit_bytes=58 * 1024 * 1024),
        cost_estimate=pl.CostEstimate(
            flops=12 * rows * keys * width // 2, bytes_accessed=6 << 20, transcendentals=rows * keys // 2
        ),
        name="attention",
    )(bounds, low, query, grad, tail, mine, other)


def rows_bounds(docs, me, span, heads):
    offset = me * span
    names = jnp.arange(8, dtype=jnp.int32)[:, None]
    starts = jnp.sum((docs[None, :] < names).astype(jnp.int32), axis=1, keepdims=True)
    part = lax.dynamic_slice_in_dim(docs, offset, span)
    low = jnp.sum(jnp.where(part[None, :] == names, starts, 0), axis=0)
    end = offset + span
    count = (end - low[0] + TILE - 1) // TILE
    base = jnp.maximum(end - count * TILE, 0)
    clear = jnp.clip((low[span - 1] - base + TILE - 1) // TILE, 0, count)
    full = jnp.clip((offset + 1 - base) // TILE, clear, count)
    limits = jnp.tile(jnp.stack([low, offset + jnp.arange(span, dtype=jnp.int32)]), (1, heads))
    return base, count, clear, full, limits


def with_partner(mask, query, grad, pair, bounds, low, width):
    ctx_size, dp_size = lax.axis_size("ctx"), lax.axis_size("dp")
    end = ctx_size - 1
    is_last = lax.axis_index("ctx") == end
    groups = [list(range(core, ctx_size, 2)) for core in range(2)]
    features = query.shape[1]

    def home(block):
        moves = [(i * ctx_size + end, (i ^ mask) * ctx_size + end) for i in range(dp_size)]
        return lax.ppermute(block, ("dp", "ctx"), moves)

    def other_core(block):
        return lax.ppermute(block, "ctx", [(i, i ^ 1) for i in range(ctx_size)])

    def same_core(blocks):
        return lax.all_to_all(blocks, "ctx", 0, 0, axis_index_groups=groups, tiled=True)

    tail = home(jnp.concatenate([query, grad, pair], axis=1))
    mine = same_core(jnp.broadcast_to(pair[None], (ctx_size // 2,) + pair.shape))
    other = other_core(mine)
    out, dquery, same, cross = attention(
        bounds, low, query, grad, tail, mine, other, width
    )
    tail = home(jnp.concatenate([out, dquery, same[-1]], axis=1))
    joint = (same.astype(jnp.float32) + other_core(cross).astype(jnp.float32)).astype(jnp.bfloat16)
    dpair = jnp.sum(same_core(joint).astype(jnp.float32), axis=0).astype(jnp.bfloat16)
    return (
        jnp.where(is_last, tail[:, :features], out),
        jnp.where(is_last, tail[:, features : 2 * features], dquery),
        jnp.where(is_last, tail[:, 2 * features :], dpair),
    )


def on_device(query_rows, key_rows, value_rows, out_grad, doc_ids, matching):
    me = lax.axis_index("ctx")
    span = query_rows.shape[1]
    width = key_rows.shape[2]
    heads = query_rows.shape[2] // width
    base, count, clear, full, low = rows_bounds(doc_ids[0], me, span, heads)
    is_last = (me == lax.axis_size("ctx") - 1).astype(jnp.int32)
    bounds = jnp.stack([base, count, clear, full, me % 2, is_last]).astype(jnp.int32)
    pair = jnp.concatenate([key_rows[0], value_rows[0]], axis=1)
    out, dquery, dpair = lax.switch(
        matching[0] - 1,
        [
            functools.partial(with_partner, mask, width=width)
            for mask in range(1, lax.axis_size("dp"))
        ],
        query_rows[0], out_grad[0], pair, bounds, low,
    )
    return out[None], dquery[None], dpair[None, :, :width], dpair[None, :, width:]


def solution(mesh):
    rows = P("dp", "ctx", None)
    return jax.shard_map(
        on_device,
        mesh=mesh,
        in_specs=(rows, rows, rows, rows, P("dp", None), P()),
        out_specs=(rows, rows, rows, rows),
        check_vma=False,
    )
```

```python
import functools
import math

import jax
import jax.numpy as jnp
from jax import lax
from jax.experimental import pallas as pl
from jax.experimental.pallas import tpu as pltpu
from jax.sharding import PartitionSpec as P

TILE = 512
LANES = 256


def dot(a, b, ca, cb):
    return lax.dot_general(a, b, (((ca,), (cb,)), ((), ())), preferred_element_type=jnp.float32)


def attention_kernel(
    heads, width, span, scale,
    device, docs, query, grad, tail, mine, other,
    results, same, cross,
    q_rows, g_rows, o_rows, g_cols, pairs, dpairs, scores, weights, dscores, out_t, dq_t, top, total, low,
    in_sem, pair_sem, out_sem,
):
    rows = heads * span
    keys = pairs.shape[0]
    groups = mine.shape[0]
    features = heads * width
    chunks = [slice(r, r + LANES) for r in range(0, rows, LANES)]
    me = device[0]
    core = lax.rem(me, 2)
    offset = me * span
    factor = scale * math.log2(math.e)

    def head_copies(wide, stacked, sem, to_stacked):
        made = []
        for h in range(heads):
            a = wide.at[:, h * width : (h + 1) * width]
            b = stacked.at[h * span : (h + 1) * span, :]
            a, b = (a, b) if to_stacked else (b, a)
            made.append(pltpu.make_async_copy(a, b, sem.at[h]))
        return made

    def block_rows(k, parity):
        return pl.ds(pl.multiple_of((2 * k + parity) * span, 32), span)

    own_q = head_copies(query, q_rows, in_sem.at[0], True)
    own_g = head_copies(grad, g_rows, in_sem.at[1], True)
    far_q = head_copies(tail.at[:, 0:features], q_rows, in_sem.at[0], True)
    far_g = head_copies(tail.at[:, features : 2 * features], g_rows, in_sem.at[1], True)
    far_pair = pltpu.make_async_copy(
        tail.at[:, 2 * features : 2 * features + 2 * width], pairs.at[keys - span : keys, :], pair_sem.at[0, groups - 1]
    )
    pair_in, pair_out = [], []
    for side, parity in enumerate((core, 1 - core)):
        for k in range(groups):
            at, sem = block_rows(k, parity), pair_sem.at[side, k]
            pair_in.append(pltpu.make_async_copy((mine, other)[side].at[k], pairs.at[at], sem))
            pair_out.append(pltpu.make_async_copy(dpairs.at[at], (same, cross)[side].at[k], sem))
    at_end = me == 2 * groups - 1

    @pl.when(at_end)
    def _():
        for c in far_q + far_g:
            c.start()
        far_pair.start()

    @pl.when(jnp.logical_not(at_end))
    def _():
        for c in own_q + own_g:
            c.start()
        pair_in[groups - 1].start()

    for i, c in enumerate(pair_in):
        if i != groups - 1:
            c.start()

    names = docs[...]
    row = pltpu.roll(names, lax.rem(keys - offset, keys), 1)[:, 0:span]
    start = jnp.zeros((1, span), jnp.int32)
    for d in range(1, 8):
        before = jnp.sum((names < d).astype(jnp.int32), axis=1, keepdims=True)
        start = jnp.where(row == d, before, start)
    place = offset + lax.broadcasted_iota(jnp.int32, (1, span), 1)
    for h in range(heads):
        low[0:1, h * span : (h + 1) * span] = start
        low[1:2, h * span : (h + 1) * span] = place
    low_first, low_last = jnp.min(start), jnp.max(start)
    end = offset + span
    count = lax.div(end - low_first + TILE - 1, TILE)
    base = jnp.maximum(end - count * TILE, 0)
    clear = jnp.minimum(lax.div(jnp.maximum(low_last - base, 0) + TILE - 1, TILE), count)
    full = jnp.minimum(jnp.maximum(lax.div(offset + 1 - base, TILE), clear), count)

    top[...] = jnp.full(top.shape, -jnp.inf, jnp.float32)
    total[...] = jnp.zeros(total.shape, jnp.float32)
    out_t[...] = jnp.zeros(out_t.shape, jnp.float32)
    dq_t[...] = jnp.zeros(dq_t.shape, jnp.float32)
    dpairs[...] = jnp.zeros(dpairs.shape, jnp.bfloat16)
    for c in own_q:
        c.wait()
    for c in pair_in:
        c.wait()

    def keys_at(t):
        return pl.ds(pl.multiple_of(base + t * TILE, 32), TILE)

    def kept_at(t):
        return pl.ds(pl.multiple_of(t * TILE, TILE), TILE)

    def score_tile(t, masked):
        key = pairs[keys_at(t), 0:width]
        for c in chunks:
            s = dot(key, q_rows[c, :], 1, 1)
            if masked:
                place = base + t * TILE + lax.broadcasted_iota(jnp.int32, (TILE, LANES), 0)
                ok = (place >= low[0:1, c]) & (place <= low[1:2, c])
                s = jnp.where(ok, s, -jnp.inf)
            scores[kept_at(t), c] = s
            top[:, c] = jnp.maximum(top[:, c], jnp.max(s.reshape(TILE // 8, 8, LANES), axis=0))

    @pl.loop(0, clear)
    def _(t):
        score_tile(t, True)

    @pl.loop(clear, full)
    def _(t):
        score_tile(t, False)

    @pl.loop(full, count)
    def _(t):
        score_tile(t, True)

    peak = jnp.max(top[...], axis=0, keepdims=True) * factor
    top[...] = jnp.broadcast_to(peak, top.shape)

    @pl.loop(0, count)
    def _(t):
        value_t = pairs[keys_at(t), width : 2 * width].T
        for c in chunks:
            p = jnp.exp2(scores[kept_at(t), c] * factor - top[0:1, c])
            total[:, c] += jnp.sum(p.reshape(TILE // 8, 8, LANES), axis=0)
            weights[kept_at(t), c] = p.astype(jnp.bfloat16)
        out_t[...] += dot(value_t, weights[kept_at(t), :], 1, 0)

    for c in own_g:
        c.wait()
    inverse = 1.0 / jnp.sum(total[...], axis=0, keepdims=True)
    for r in range(0, rows, 128):
        c = slice(r, r + 128)
        o = out_t[:, c] * inverse[:, c]
        g = (g_rows[c, :].T.astype(jnp.float32) * inverse[:, c]).astype(jnp.bfloat16)
        g_cols[:, c] = g
        top[0:1, c] = jnp.sum(g.astype(jnp.float32) * o, axis=0, keepdims=True)
        o_rows[c, :] = o.T.astype(jnp.bfloat16)
    out_copies = head_copies(results.at[:, 0:features], o_rows, out_sem.at[0], False)
    for c in out_copies:
        c.start()

    @pl.loop(0, count)
    def _(t):
        at = keys_at(t)
        kept = kept_at(t)
        key = pairs[at, 0:width]
        key_t = key.T
        value = pairs[at, width : 2 * width]
        dv = dot(weights[kept, :], g_cols[...], 1, 1)
        dpairs[at, width : 2 * width] = dv.astype(jnp.bfloat16)
        for c in chunks:
            dp = dot(value, g_cols[:, c], 1, 0)
            dscores[:, c] = weights[kept, c] * (dp - top[0:1, c]).astype(jnp.bfloat16)
        dk = dot(dscores[...], q_rows[...], 1, 0)
        dpairs[at, 0:width] = (dk * scale).astype(jnp.bfloat16)
        dq_t[...] += dot(key_t, dscores[...], 1, 0)

    for c in pair_out:
        c.start()
    tail_out = pltpu.make_async_copy(
        dpairs.at[keys - span : keys, :],
        results.at[:, 2 * features : 2 * features + 2 * width],
        in_sem.at[0, 0],
    )
    tail_out.start()
    for r in range(0, rows, 128):
        g_rows[r : r + 128, :] = (dq_t[:, r : r + 128].T * scale).astype(jnp.bfloat16)
    last_copies = head_copies(results.at[:, features : 2 * features], g_rows, out_sem.at[1], False)
    for c in last_copies:
        c.start()
    for c in out_copies + pair_out + last_copies + [tail_out]:
        c.wait()


def attention(device, docs, query, grad, tail, mine, other, width):
    span, features = query.shape
    heads = features // width
    groups = mine.shape[0]
    rows, keys = heads * span, 2 * groups * span
    kernel = functools.partial(attention_kernel, heads, width, span, 1.0 / math.sqrt(width))
    vmem, hbm = pl.BlockSpec(memory_space=pltpu.VMEM), pl.BlockSpec(memory_space=pl.ANY)
    bf16, f32 = jnp.bfloat16, jnp.float32
    return pl.pallas_call(
        kernel,
        out_shape=(
            jax.ShapeDtypeStruct(tail.shape, bf16),
            jax.ShapeDtypeStruct(mine.shape, bf16),
            jax.ShapeDtypeStruct(mine.shape, bf16),
        ),
        in_specs=[pl.BlockSpec(memory_space=pltpu.SMEM), vmem] + [hbm] * 5,
        out_specs=(hbm,) * 3,
        scratch_shapes=[
            pltpu.VMEM((rows, width), bf16),
            pltpu.VMEM((rows, width), bf16),
            pltpu.VMEM((rows, width), bf16),
            pltpu.VMEM((width, rows), bf16),
            pltpu.VMEM((keys, 2 * width), bf16),
            pltpu.VMEM((keys, 2 * width), bf16),
            pltpu.VMEM((keys, rows), f32),
            pltpu.VMEM((keys, rows), bf16),
            pltpu.VMEM((TILE, rows), bf16),
            pltpu.VMEM((width, rows), f32),
            pltpu.VMEM((width, rows), f32),
            pltpu.VMEM((8, rows), f32),
            pltpu.VMEM((8, rows), f32),
            pltpu.VMEM((8, rows), jnp.int32),
            pltpu.SemaphoreType.DMA((2, heads)),
            pltpu.SemaphoreType.DMA((2, groups)),
            pltpu.SemaphoreType.DMA((2, heads)),
        ],
        compiler_params=pltpu.CompilerParams(vmem_limit_bytes=58 * 1024 * 1024),
        cost_estimate=pl.CostEstimate(
            flops=12 * rows * keys * width // 2, bytes_accessed=6 << 20, transcendentals=rows * keys // 2
        ),
        name="attention",
    )(device, docs, query, grad, tail, mine, other)


def home_moves(mask):
    ctx_size, dp_size = lax.axis_size("ctx"), lax.axis_size("dp")
    end = ctx_size - 1
    moves = [(i * ctx_size + end, (i ^ mask) * ctx_size + end) for i in range(dp_size)]
    return lambda block: lax.ppermute(block, ("dp", "ctx"), moves)


def other_core(block):
    return lax.ppermute(block, "ctx", [(i, i ^ 1) for i in range(lax.axis_size("ctx"))])


def same_core(blocks):
    groups = [list(range(core, lax.axis_size("ctx"), 2)) for core in range(2)]
    return lax.all_to_all(blocks, "ctx", 0, 0, axis_index_groups=groups, tiled=True)


def gather(mask, query, grad, key, value):
    pair = jnp.concatenate([key, value], axis=1)
    tail = home_moves(mask)(jnp.concatenate([query, grad, pair], axis=1))
    mine = same_core(jnp.broadcast_to(pair[None], (lax.axis_size("ctx") // 2,) + pair.shape))
    return tail, mine, other_core(mine)


def reduce(mask, results, same, cross):
    tail = home_moves(mask)(results)
    joint = (same.astype(jnp.float32) + other_core(cross).astype(jnp.float32)).astype(jnp.bfloat16)
    return tail, same_core(joint)


def on_device(query_rows, key_rows, value_rows, out_grad, doc_ids, matching):
    width, features = key_rows.shape[2], query_rows.shape[2]
    masks = range(1, lax.axis_size("dp"))
    is_last = lax.axis_index("ctx") == lax.axis_size("ctx") - 1
    query, grad = query_rows[0], out_grad[0]
    tail, mine, other = lax.switch(
        matching[0] - 1,
        [functools.partial(gather, mask) for mask in masks],
        query, grad, key_rows[0], value_rows[0],
    )
    device = lax.axis_index("ctx").astype(jnp.int32)[None]
    results, same, cross = attention(device, doc_ids, query, grad, tail, mine, other, width)
    tail, terms = lax.switch(
        matching[0] - 1, [functools.partial(reduce, mask) for mask in masks], results, same, cross
    )
    dpair = jnp.sum(terms.astype(jnp.float32), axis=0).astype(jnp.bfloat16)
    edges = [0, features, 2 * features, 2 * features + width, 2 * features + 2 * width]
    own = [results[:, :features], results[:, features : 2 * features], dpair[:, :width], dpair[:, width:]]
    return tuple(
        jnp.where(is_last, tail[:, a:b], o)[None] for a, b, o in zip(edges[:-1], edges[1:], own)
    )


def solution(mesh):
    rows = P("dp", "ctx", None)
    return jax.shard_map(
        on_device,
        mesh=mesh,
        in_specs=(rows, rows, rows, rows, P("dp", None), P()),
        out_specs=(rows, rows, rows, rows),
        check_vma=False,
    )
```

```python
import functools
import math

import jax
import jax.numpy as jnp
from jax import lax
from jax.experimental import pallas as pl
from jax.experimental.pallas import tpu as pltpu
from jax.sharding import PartitionSpec as P

TILE = 512
LANES = 256


def dot(a, b, ca, cb):
    return lax.dot_general(a, b, (((ca,), (cb,)), ((), ())), preferred_element_type=jnp.float32)


def attention_kernel(
    heads, width, span, scale,
    device, docs, query, grad, gathered,
    out, dquery, terms,
    q_rows, g_rows, o_rows, g_cols, pairs, dpairs, scores, weights, dscores, out_t, dq_t, top, total, low,
    in_sem, pair_sem, out_sem,
):
    rows = heads * span
    keys = pairs.shape[0]
    chunks = [slice(r, r + LANES) for r in range(0, rows, LANES)]
    me = device[0]
    offset = me * span
    factor = scale * math.log2(math.e)

    def head_copies(wide, stacked, sem, to_stacked):
        made = []
        for h in range(heads):
            a = wide.at[:, h * width : (h + 1) * width]
            b = stacked.at[h * span : (h + 1) * span, :]
            a, b = (a, b) if to_stacked else (b, a)
            made.append(pltpu.make_async_copy(a, b, sem.at[h]))
        return made

    own_q = head_copies(query, q_rows, in_sem.at[0], True)
    own_g = head_copies(grad, g_rows, in_sem.at[1], True)
    pair_in = pltpu.make_async_copy(gathered, pairs, pair_sem.at[0])
    for c in own_q + [pair_in] + own_g:
        c.start()

    names = docs[...]
    row = pltpu.roll(names, lax.rem(keys - offset, keys), 1)[:, 0:span]
    start = jnp.zeros((1, span), jnp.int32)
    for d in range(1, 8):
        before = jnp.sum((names < d).astype(jnp.int32), axis=1, keepdims=True)
        start = jnp.where(row == d, before, start)
    place = offset + lax.broadcasted_iota(jnp.int32, (1, span), 1)
    for h in range(heads):
        low[0:1, h * span : (h + 1) * span] = start
        low[1:2, h * span : (h + 1) * span] = place
    low_first, low_last = jnp.min(start), jnp.max(start)
    end = offset + span
    count = lax.div(end - low_first + TILE - 1, TILE)
    base = jnp.maximum(end - count * TILE, 0)
    clear = jnp.minimum(lax.div(jnp.maximum(low_last - base, 0) + TILE - 1, TILE), count)
    full = jnp.minimum(jnp.maximum(lax.div(offset + 1 - base, TILE), clear), count)

    top[...] = jnp.full(top.shape, -jnp.inf, jnp.float32)
    total[...] = jnp.zeros(total.shape, jnp.float32)
    out_t[...] = jnp.zeros(out_t.shape, jnp.float32)
    dq_t[...] = jnp.zeros(dq_t.shape, jnp.float32)
    dpairs[...] = jnp.zeros(dpairs.shape, jnp.bfloat16)
    for c in own_q + [pair_in]:
        c.wait()

    def keys_at(t):
        return pl.ds(pl.multiple_of(base + t * TILE, 32), TILE)

    def kept_at(t):
        return pl.ds(pl.multiple_of(t * TILE, TILE), TILE)

    def score_tile(t, masked):
        key = pairs[keys_at(t), 0:width]
        for c in chunks:
            s = dot(key, q_rows[c, :], 1, 1)
            if masked:
                place = base + t * TILE + lax.broadcasted_iota(jnp.int32, (TILE, LANES), 0)
                ok = (place >= low[0:1, c]) & (place <= low[1:2, c])
                s = jnp.where(ok, s, -jnp.inf)
            scores[kept_at(t), c] = s
            top[:, c] = jnp.maximum(top[:, c], jnp.max(s.reshape(TILE // 8, 8, LANES), axis=0))

    @pl.loop(0, clear)
    def _(t):
        score_tile(t, True)

    @pl.loop(clear, full)
    def _(t):
        score_tile(t, False)

    @pl.loop(full, count)
    def _(t):
        score_tile(t, True)

    peak = jnp.max(top[...], axis=0, keepdims=True) * factor
    top[...] = jnp.broadcast_to(peak, top.shape)

    @pl.loop(0, count)
    def _(t):
        value_t = pairs[keys_at(t), width : 2 * width].T
        for c in chunks:
            p = jnp.exp2(scores[kept_at(t), c] * factor - top[0:1, c])
            total[:, c] += jnp.sum(p.reshape(TILE // 8, 8, LANES), axis=0)
            weights[kept_at(t), c] = p.astype(jnp.bfloat16)
        out_t[...] += dot(value_t, weights[kept_at(t), :], 1, 0)

    for c in own_g:
        c.wait()
    inverse = 1.0 / jnp.sum(total[...], axis=0, keepdims=True)
    for r in range(0, rows, 128):
        c = slice(r, r + 128)
        o = out_t[:, c] * inverse[:, c]
        g = (g_rows[c, :].T.astype(jnp.float32) * inverse[:, c]).astype(jnp.bfloat16)
        g_cols[:, c] = g
        top[0:1, c] = jnp.sum(g.astype(jnp.float32) * o, axis=0, keepdims=True)
        o_rows[c, :] = o.T.astype(jnp.bfloat16)
    out_copies = head_copies(out, o_rows, out_sem.at[0], False)
    for c in out_copies:
        c.start()

    @pl.loop(0, count)
    def _(t):
        at = keys_at(t)
        kept = kept_at(t)
        key = pairs[at, 0:width]
        key_t = key.T
        value = pairs[at, width : 2 * width]
        dv = dot(weights[kept, :], g_cols[...], 1, 1)
        dpairs[at, width : 2 * width] = dv.astype(jnp.bfloat16)
        for c in chunks:
            dp = dot(value, g_cols[:, c], 1, 0)
            dscores[:, c] = weights[kept, c] * (dp - top[0:1, c]).astype(jnp.bfloat16)
        dk = dot(dscores[...], q_rows[...], 1, 0)
        dpairs[at, 0:width] = (dk * scale).astype(jnp.bfloat16)
        dq_t[...] += dot(key_t, dscores[...], 1, 0)

    pair_out = pltpu.make_async_copy(dpairs, terms, pair_sem.at[1])
    pair_out.start()
    for r in range(0, rows, 128):
        g_rows[r : r + 128, :] = (dq_t[:, r : r + 128].T * scale).astype(jnp.bfloat16)
    last_copies = head_copies(dquery, g_rows, out_sem.at[1], False)
    for c in last_copies:
        c.start()
    for c in out_copies + [pair_out] + last_copies:
        c.wait()


def attention(device, docs, query, grad, gathered, width):
    span, features = query.shape
    heads = features // width
    rows, keys = heads * span, gathered.shape[0]
    kernel = functools.partial(attention_kernel, heads, width, span, 1.0 / math.sqrt(width))
    vmem, hbm = pl.BlockSpec(memory_space=pltpu.VMEM), pl.BlockSpec(memory_space=pl.ANY)
    bf16, f32 = jnp.bfloat16, jnp.float32
    return pl.pallas_call(
        kernel,
        out_shape=(
            jax.ShapeDtypeStruct((span, features), bf16),
            jax.ShapeDtypeStruct((span, features), bf16),
            jax.ShapeDtypeStruct(gathered.shape, bf16),
        ),
        in_specs=[pl.BlockSpec(memory_space=pltpu.SMEM), vmem] + [hbm] * 3,
        out_specs=(hbm,) * 3,
        scratch_shapes=[
            pltpu.VMEM((rows, width), bf16),
            pltpu.VMEM((rows, width), bf16),
            pltpu.VMEM((rows, width), bf16),
            pltpu.VMEM((width, rows), bf16),
            pltpu.VMEM((keys, 2 * width), bf16),
            pltpu.VMEM((keys, 2 * width), bf16),
            pltpu.VMEM((keys, rows), f32),
            pltpu.VMEM((keys, rows), bf16),
            pltpu.VMEM((TILE, rows), bf16),
            pltpu.VMEM((width, rows), f32),
            pltpu.VMEM((width, rows), f32),
            pltpu.VMEM((8, rows), f32),
            pltpu.VMEM((8, rows), f32),
            pltpu.VMEM((8, rows), jnp.int32),
            pltpu.SemaphoreType.DMA((2, heads)),
            pltpu.SemaphoreType.DMA((2,)),
            pltpu.SemaphoreType.DMA((2, heads)),
        ],
        compiler_params=pltpu.CompilerParams(vmem_limit_bytes=58 * 1024 * 1024),
        cost_estimate=pl.CostEstimate(
            flops=12 * rows * keys * width // 2, bytes_accessed=6 << 20, transcendentals=rows * keys // 2
        ),
        name="attention",
    )(device, docs, query, grad, gathered)


def across(block, matching, dp_size):
    def turn(mask):
        return lambda v: lax.ppermute(v, "dp", [(i, i ^ mask) for i in range(dp_size)])

    return lax.switch(matching[0] - 1, [turn(mask) for mask in range(1, dp_size)], block)


def on_device(query_rows, key_rows, value_rows, out_grad, doc_ids, matching):
    ctx_size, dp_size = lax.axis_size("ctx"), lax.axis_size("dp")
    me = lax.axis_index("ctx")
    span, width = key_rows.shape[1:]
    is_last = me == ctx_size - 1
    stored = jnp.concatenate([key_rows[0], value_rows[0]], axis=1)
    names = doc_ids.astype(jnp.bfloat16).reshape(-1, 2 * width)
    names = jnp.pad(names, ((0, -names.shape[0] % 16), (0, 0)))
    arrived = across(jnp.concatenate([stored, names], axis=0), matching, dp_size)
    to_last = jnp.where(is_last, stored, arrived[:span])
    sending = jnp.concatenate(
        [jnp.broadcast_to(stored[None], (ctx_size - 1,) + stored.shape), to_last[None]], axis=0
    )
    gathered = lax.all_to_all(sending, "ctx", 0, 0).reshape(ctx_size * span, 2 * width)
    count = doc_ids.shape[1] // (2 * width)
    far = arrived[span : span + count].reshape(1, -1).astype(jnp.int32)
    docs = jnp.where(is_last, far, doc_ids)
    out, dquery, terms = attention(
        me.astype(jnp.int32)[None], docs, query_rows[0], out_grad[0], gathered, width
    )
    terms = lax.all_to_all(terms.reshape(ctx_size, span, 2 * width), "ctx", 0, 0)
    tail = terms[ctx_size - 1]
    back = across(tail, matching, dp_size).astype(jnp.float32)
    own = jnp.sum(terms[: ctx_size - 1].astype(jnp.float32), axis=0)
    final = jnp.where(is_last, tail.astype(jnp.float32), own + back).astype(jnp.bfloat16)
    return out[None], dquery[None], final[None, :, :width], final[None, :, width:]


def solution(mesh):
    rows = P("dp", "ctx", None)
    return jax.shard_map(
        on_device,
        mesh=mesh,
        in_specs=(rows, rows, rows, rows, P("dp", None), P()),
        out_specs=(rows, rows, rows, rows),
        check_vma=False,
    )
```

```python
import functools
import math

import jax
import jax.numpy as jnp
from jax import lax
from jax.experimental import pallas as pl
from jax.experimental.pallas import tpu as pltpu
from jax.sharding import PartitionSpec as P

TILE = 512
LANES = 256
BF16, F32, I32 = jnp.bfloat16, jnp.float32, jnp.int32


def dot(a, b, ca, cb):
    return lax.dot_general(a, b, (((ca,), (cb,)), ((), ())), preferred_element_type=F32)


def head_copies(wide, stacked, sem, to_stacked):
    span, width = wide.shape[0], stacked.shape[1]
    made = []
    for h in range(wide.shape[1] // width):
        a = wide.at[:, h * width : (h + 1) * width]
        b = stacked.at[h * span : (h + 1) * span, :]
        a, b = (a, b) if to_stacked else (b, a)
        made.append(pltpu.make_async_copy(a, b, sem.at[h]))
    return made


def begin(copies):
    for c in copies:
        c.start()


def finish(copies):
    for c in copies:
        c.wait()


def kept_at(t):
    return pl.ds(pl.multiple_of(t * TILE, TILE), TILE)


def softmax_kernel(
    span, scale,
    device, docs, query, keys_in,
    probs, total, bounds,
    q_rows, keys, scores, weights, top, low, in_sem, key_sem, out_sem,
):
    rows, width = q_rows.shape
    key_count = keys.shape[0]
    heads = rows // span
    chunks = [slice(r, r + LANES) for r in range(0, rows, LANES)]
    factor = scale * math.log2(math.e)
    offset = device[0] * span

    arriving = head_copies(query, q_rows, in_sem, True)
    arriving.append(pltpu.make_async_copy(keys_in, keys, key_sem))
    begin(arriving)

    names = docs[...]
    row = pltpu.roll(names, lax.rem(key_count - offset, key_count), 1)[:, 0:span]
    start = jnp.zeros((1, span), I32)
    for d in range(1, 8):
        before = jnp.sum((names < d).astype(I32), axis=1, keepdims=True)
        start = jnp.where(row == d, before, start)
    place = offset + lax.broadcasted_iota(I32, (1, span), 1)
    for h in range(heads):
        low[0:1, h * span : (h + 1) * span] = start
        low[1:2, h * span : (h + 1) * span] = place
    low_first, low_last = jnp.min(start), jnp.max(start)
    end = offset + span
    count = lax.div(end - low_first + TILE - 1, TILE)
    base = jnp.maximum(end - count * TILE, 0)
    clear = jnp.minimum(lax.div(jnp.maximum(low_last - base, 0) + TILE - 1, TILE), count)
    full = jnp.minimum(jnp.maximum(lax.div(offset + 1 - base, TILE), clear), count)
    bounds[0] = base
    bounds[1] = count

    top[...] = jnp.full(top.shape, -jnp.inf, F32)
    total[...] = jnp.zeros(total.shape, F32)
    finish(arriving)

    def score_tile(t, masked):
        key = keys[pl.ds(pl.multiple_of(base + t * TILE, 32), TILE), :]
        for c in chunks:
            s = dot(key, q_rows[c, :], 1, 1)
            if masked:
                at = base + t * TILE + lax.broadcasted_iota(I32, (TILE, LANES), 0)
                ok = (at >= low[0:1, c]) & (at <= low[1:2, c])
                s = jnp.where(ok, s, -jnp.inf)
            scores[kept_at(t), c] = s
            top[:, c] = jnp.maximum(top[:, c], jnp.max(s.reshape(TILE // 8, 8, LANES), axis=0))

    @pl.loop(0, clear)
    def _(t):
        score_tile(t, True)

    @pl.loop(clear, full)
    def _(t):
        score_tile(t, False)

    @pl.loop(full, count)
    def _(t):
        score_tile(t, True)

    peak = jnp.max(top[...], axis=0, keepdims=True) * factor
    top[...] = jnp.broadcast_to(peak, top.shape)

    def leaving(t):
        return pltpu.make_async_copy(weights.at[kept_at(t)], probs.at[kept_at(t)], out_sem.at[t])

    @pl.loop(0, count)
    def _(t):
        for c in chunks:
            p = jnp.exp2(scores[kept_at(t), c] * factor - top[0:1, c])
            total[:, c] += jnp.sum(p.reshape(TILE // 8, 8, LANES), axis=0)
            weights[kept_at(t), c] = p.astype(BF16)
        leaving(t).start()

    @pl.loop(0, count)
    def _(t):
        leaving(t).wait()


def output_kernel(
    bounds, total, grad, values_in, probs,
    out, g_cols, delta, dvalues_out,
    g_rows, o_rows, values, dvalues, weights, out_t, in_sem, value_sem, prob_sem, out_sem,
):
    rows, width = g_rows.shape
    base, count = bounds[0], bounds[1]

    def arriving(t):
        return pltpu.make_async_copy(probs.at[kept_at(t)], weights.at[kept_at(t)], prob_sem.at[t])

    values_copy = pltpu.make_async_copy(values_in, values, value_sem)
    values_copy.start()

    @pl.loop(0, count)
    def _(t):
        arriving(t).start()

    grad_copies = head_copies(grad, g_rows, in_sem, True)
    begin(grad_copies)
    out_t[...] = jnp.zeros(out_t.shape, F32)
    dvalues[...] = jnp.zeros(dvalues.shape, BF16)
    inverse = 1.0 / jnp.sum(total[...], axis=0, keepdims=True)
    finish(grad_copies)
    for r in range(0, rows, 128):
        c = slice(r, r + 128)
        g_cols[:, c] = (g_rows[c, :].T.astype(F32) * inverse[:, c]).astype(BF16)
    values_copy.wait()

    def keys_at(t):
        return pl.ds(pl.multiple_of(base + t * TILE, 32), TILE)

    @pl.loop(0, count)
    def _(t):
        arriving(t).wait()
        value_t = values[keys_at(t), :].T
        out_t[...] += dot(value_t, weights[kept_at(t), :], 1, 0)
        dvalues[keys_at(t), :] = dot(weights[kept_at(t), :], g_cols[...], 1, 1).astype(BF16)

    leaving = [pltpu.make_async_copy(dvalues, dvalues_out, value_sem)]
    begin(leaving)
    for r in range(0, rows, 128):
        c = slice(r, r + 128)
        o = out_t[:, c] * inverse[:, c]
        delta[0:1, c] = jnp.sum(g_cols[:, c].astype(F32) * o, axis=0, keepdims=True)
        o_rows[c, :] = o.T.astype(BF16)
    out_copies = head_copies(out, o_rows, out_sem, False)
    begin(out_copies)
    finish(leaving + out_copies)


def gradient_kernel(
    scale,
    bounds, g_cols, delta, query, keys_in, values_in, probs,
    dquery, dkeys_out,
    q_rows, keys, values, dkeys, weights, dscores, dq_t, in_sem, pair_sem, prob_sem, out_sem,
):
    rows, width = q_rows.shape
    chunks = [slice(r, r + LANES) for r in range(0, rows, LANES)]
    base, count = bounds[0], bounds[1]

    def arriving(t):
        return pltpu.make_async_copy(probs.at[kept_at(t)], weights.at[kept_at(t)], prob_sem.at[t])

    pair_copies = [
        pltpu.make_async_copy(values_in, values, pair_sem.at[0]),
        pltpu.make_async_copy(keys_in, keys, pair_sem.at[1]),
    ]
    begin(pair_copies)

    @pl.loop(0, count)
    def _(t):
        arriving(t).start()

    query_copies = head_copies(query, q_rows, in_sem, True)
    begin(query_copies)
    dq_t[...] = jnp.zeros(dq_t.shape, F32)
    dkeys[...] = jnp.zeros(dkeys.shape, BF16)
    finish(pair_copies + query_copies)

    @pl.loop(0, count)
    def _(t):
        at = pl.ds(pl.multiple_of(base + t * TILE, 32), TILE)
        kept = kept_at(t)
        arriving(t).wait()
        value = values[at, :]
        for c in chunks:
            dp = dot(value, g_cols[:, c], 1, 0)
            dscores[:, c] = weights[kept, c] * (dp - delta[0:1, c]).astype(BF16)
        dk = dot(dscores[...], q_rows[...], 1, 0)
        dkeys[at, :] = (dk * scale).astype(BF16)
        dq_t[...] += dot(keys[at, :].T, dscores[...], 1, 0)

    leaving = [pltpu.make_async_copy(dkeys, dkeys_out, pair_sem.at[0])]
    begin(leaving)
    for r in range(0, rows, 128):
        q_rows[r : r + 128, :] = (dq_t[:, r : r + 128].T * scale).astype(BF16)
    out_copies = head_copies(dquery, q_rows, out_sem, False)
    begin(out_copies)
    finish(leaving + out_copies)


VMEM = pl.BlockSpec(memory_space=pltpu.VMEM)
SMEM = pl.BlockSpec(memory_space=pltpu.SMEM)
HBM = pl.BlockSpec(memory_space=pl.ANY)


def call(kernel, name, products, sizes, in_specs, outs, scratch):
    rows, keys, width = sizes
    return pl.pallas_call(
        kernel,
        out_shape=tuple(jax.ShapeDtypeStruct(shape, dtype) for shape, dtype, _ in outs),
        in_specs=in_specs,
        out_specs=tuple(spec for _, _, spec in outs),
        scratch_shapes=scratch,
        compiler_params=pltpu.CompilerParams(vmem_limit_bytes=50 * 1024 * 1024),
        cost_estimate=pl.CostEstimate(
            flops=products * 3 * rows * keys * width, bytes_accessed=20 << 20, transcendentals=0
        ),
        name=name,
    )


def local(device, docs, query, grad, all_keys, all_values, exchange):
    span, features = query.shape
    keys, width = all_keys.shape
    heads = features // width
    rows, most = heads * span, keys // TILE
    sizes = (rows, keys, width)
    scale = 1.0 / math.sqrt(width)
    dma = pltpu.SemaphoreType.DMA
    probs, total, bounds = call(
        functools.partial(softmax_kernel, span, scale), "softmax", 1, sizes,
        [SMEM, VMEM, HBM, HBM],
        [((keys, rows), BF16, HBM), ((8, rows), F32, VMEM), ((2,), I32, SMEM)],
        [
            pltpu.VMEM((rows, width), BF16), pltpu.VMEM((keys, width), BF16),
            pltpu.VMEM((keys, rows), F32), pltpu.VMEM((keys, rows), BF16),
            pltpu.VMEM((8, rows), F32), pltpu.VMEM((8, rows), I32),
            dma((heads,)), dma, dma((most,)),
        ],
    )(device, docs, query, all_keys)
    out, g_cols, delta, dvalues = call(
        output_kernel, "output", 2, sizes,
        [SMEM, VMEM, HBM, HBM, HBM],
        [
            ((span, features), BF16, HBM), ((width, rows), BF16, VMEM),
            ((8, rows), F32, VMEM), ((keys, width), BF16, HBM),
        ],
        [
            pltpu.VMEM((rows, width), BF16), pltpu.VMEM((rows, width), BF16),
            pltpu.VMEM((keys, width), BF16), pltpu.VMEM((keys, width), BF16),
            pltpu.VMEM((keys, rows), BF16), pltpu.VMEM((width, rows), F32),
            dma((heads,)), dma, dma((most,)), dma((heads,)),
        ],
    )(bounds, total, grad, all_values, probs)
    dvalue_terms = exchange(dvalues)
    dquery, dkeys = call(
        functools.partial(gradient_kernel, scale), "gradient", 3, sizes,
        [SMEM, VMEM, VMEM, HBM, HBM, HBM, HBM],
        [((span, features), BF16, HBM), ((keys, width), BF16, HBM)],
        [
            pltpu.VMEM((rows, width), BF16), pltpu.VMEM((keys, width), BF16),
            pltpu.VMEM((keys, width), BF16), pltpu.VMEM((keys, width), BF16),
            pltpu.VMEM((keys, rows), BF16), pltpu.VMEM((TILE, rows), BF16),
            pltpu.VMEM((width, rows), F32),
            dma((heads,)), dma((2,)), dma((most,)), dma((heads,)),
        ],
    )(bounds, g_cols, delta, query, all_keys, all_values, probs)
    return out, dquery, dkeys, dvalue_terms


def across(block, matching, dp_size):
    def turn(mask):
        return lambda v: lax.ppermute(v, "dp", [(i, i ^ mask) for i in range(dp_size)])

    return lax.switch(matching[0] - 1, [turn(mask) for mask in range(1, dp_size)], block)


def on_device(query_rows, key_rows, value_rows, out_grad, doc_ids, matching):
    ctx_size, dp_size = lax.axis_size("ctx"), lax.axis_size("dp")
    me = lax.axis_index("ctx")
    span, width = key_rows.shape[1:]
    keys = ctx_size * span
    is_last = me == ctx_size - 1
    stored = jnp.concatenate([key_rows[0], value_rows[0]], axis=1)
    names = doc_ids.astype(BF16).reshape(-1, 2 * width)
    names = jnp.pad(names, ((0, -names.shape[0] % 16), (0, 0)))
    arrived = across(jnp.concatenate([stored, names], axis=0), matching, dp_size)

    def exchange(blocks):
        return lax.all_to_all(blocks, "ctx", 0, 0)

    def exchange_rows(terms):
        return exchange(terms.reshape(ctx_size, span, width))

    def gather(own, part):
        last = jnp.where(is_last, own, arrived[:span, part])
        which = lax.broadcasted_iota(I32, (ctx_size, 1, 1), 0) == ctx_size - 1
        return exchange(jnp.where(which, last[None], own[None])).reshape(keys, width)

    all_keys = gather(key_rows[0], slice(0, width))
    all_values = gather(value_rows[0], slice(width, 2 * width))
    doc_rows = doc_ids.shape[1] // (2 * width)
    far = arrived[span : span + doc_rows].reshape(1, -1).astype(I32)
    docs = jnp.where(is_last, far, doc_ids)
    out, dquery, dkeys, dvalue_terms = local(
        me.astype(I32)[None], docs, query_rows[0], out_grad[0], all_keys, all_values, exchange_rows
    )
    dkey_terms = exchange_rows(dkeys)
    both = (dkey_terms, dvalue_terms)
    tail = jnp.concatenate([terms[ctx_size - 1] for terms in both], axis=1)
    back = across(tail, matching, dp_size)

    def final(terms, part):
        own = jnp.sum(terms[: ctx_size - 1].astype(F32), axis=0) + back[:, part].astype(F32)
        return jnp.where(is_last, terms[ctx_size - 1].astype(F32), own).astype(BF16)[None]

    return (
        out[None],
        dquery[None],
        final(dkey_terms, slice(0, width)),
        final(dvalue_terms, slice(width, 2 * width)),
    )


def solution(mesh):
    rows = P("dp", "ctx", None)
    return jax.shard_map(
        on_device,
        mesh=mesh,
        in_specs=(rows, rows, rows, rows, P("dp", None), P()),
        out_specs=(rows, rows, rows, rows),
        check_vma=False,
    )
```

```python
import functools
import math

import jax
import jax.numpy as jnp
from jax import lax
from jax.experimental import pallas as pl
from jax.experimental.pallas import tpu as pltpu
from jax.sharding import PartitionSpec as P

TILE = 512
LANES = 256
BF16, F32, I32 = jnp.bfloat16, jnp.float32, jnp.int32


def dot(a, b, ca, cb):
    return lax.dot_general(a, b, (((ca,), (cb,)), ((), ())), preferred_element_type=F32)


def head_copies(wide, stacked, sem, to_stacked):
    span, width = wide.shape[0], stacked.shape[1]
    made = []
    for h in range(wide.shape[1] // width):
        a = wide.at[:, h * width : (h + 1) * width]
        b = stacked.at[h * span : (h + 1) * span, :]
        a, b = (a, b) if to_stacked else (b, a)
        made.append(pltpu.make_async_copy(a, b, sem.at[h]))
    return made


def begin(copies):
    for c in copies:
        c.start()


def finish(copies):
    for c in copies:
        c.wait()


def kept_at(t):
    return pl.ds(pl.multiple_of(t * TILE, TILE), TILE)


def forward_kernel(
    span, scale,
    device, docs, query, grad, pairs,
    out, probs, g_cols, delta, bounds, dvalues_out,
    q_rows, g_rows, o_rows, dvalues, scores, weights, out_t, top, total, low,
    in_sem, pair_sem, prob_sem, out_sem,
):
    rows, width = q_rows.shape
    key_count = pairs.shape[0]
    heads = rows // span
    chunks = [slice(r, r + LANES) for r in range(0, rows, LANES)]
    factor = scale * math.log2(math.e)
    offset = device[0] * span

    arriving = head_copies(query, q_rows, in_sem.at[0], True)
    grad_copies = head_copies(grad, g_rows, in_sem.at[1], True)
    begin(arriving + grad_copies)

    names = docs[...]
    row = pltpu.roll(names, lax.rem(key_count - offset, key_count), 1)[:, 0:span]
    start = jnp.zeros((1, span), I32)
    for d in range(1, 8):
        before = jnp.sum((names < d).astype(I32), axis=1, keepdims=True)
        start = jnp.where(row == d, before, start)
    place = offset + lax.broadcasted_iota(I32, (1, span), 1)
    for h in range(heads):
        low[0:1, h * span : (h + 1) * span] = start
        low[1:2, h * span : (h + 1) * span] = place
    low_first, low_last = jnp.min(start), jnp.max(start)
    end = offset + span
    count = lax.div(end - low_first + TILE - 1, TILE)
    base = jnp.maximum(end - count * TILE, 0)
    clear = jnp.minimum(lax.div(jnp.maximum(low_last - base, 0) + TILE - 1, TILE), count)
    full = jnp.minimum(jnp.maximum(lax.div(offset + 1 - base, TILE), clear), count)
    bounds[0] = base
    bounds[1] = count

    top[...] = jnp.full(top.shape, -jnp.inf, F32)
    total[...] = jnp.zeros(total.shape, F32)
    out_t[...] = jnp.zeros(out_t.shape, F32)
    dvalues[...] = jnp.zeros(dvalues.shape, BF16)
    finish(arriving)

    def keys_at(t):
        return pl.ds(pl.multiple_of(base + t * TILE, 32), TILE)

    def score_tile(t, masked):
        key = pairs[keys_at(t), 0:width]
        for c in chunks:
            s = dot(key, q_rows[c, :], 1, 1)
            if masked:
                at = base + t * TILE + lax.broadcasted_iota(I32, (TILE, LANES), 0)
                ok = (at >= low[0:1, c]) & (at <= low[1:2, c])
                s = jnp.where(ok, s, -jnp.inf)
            scores[kept_at(t), c] = s
            top[:, c] = jnp.maximum(top[:, c], jnp.max(s.reshape(TILE // 8, 8, LANES), axis=0))

    @pl.loop(0, clear)
    def _(t):
        score_tile(t, True)

    @pl.loop(clear, full)
    def _(t):
        score_tile(t, False)

    @pl.loop(full, count)
    def _(t):
        score_tile(t, True)

    peak = jnp.max(top[...], axis=0, keepdims=True) * factor
    top[...] = jnp.broadcast_to(peak, top.shape)

    def leaving(t):
        return pltpu.make_async_copy(weights.at[kept_at(t)], probs.at[kept_at(t)], prob_sem.at[t])

    @pl.loop(0, count)
    def _(t):
        value_t = pairs[keys_at(t), width : 2 * width].T
        for c in chunks:
            p = jnp.exp2(scores[kept_at(t), c] * factor - top[0:1, c])
            total[:, c] += jnp.sum(p.reshape(TILE // 8, 8, LANES), axis=0)
            weights[kept_at(t), c] = p.astype(BF16)
        leaving(t).start()
        out_t[...] += dot(value_t, weights[kept_at(t), :], 1, 0)

    finish(grad_copies)
    inverse = 1.0 / jnp.sum(total[...], axis=0, keepdims=True)
    for r in range(0, rows, 128):
        c = slice(r, r + 128)
        o = out_t[:, c] * inverse[:, c]
        g = (g_rows[c, :].T.astype(F32) * inverse[:, c]).astype(BF16)
        g_cols[:, c] = g
        delta[0:1, c] = jnp.sum(g.astype(F32) * o, axis=0, keepdims=True)
        o_rows[c, :] = o.T.astype(BF16)
    out_copies = head_copies(out, o_rows, out_sem, False)
    begin(out_copies)

    @pl.loop(0, count)
    def _(t):
        dvalues[keys_at(t), :] = dot(weights[kept_at(t), :], g_cols[...], 1, 1).astype(BF16)

    values_copy = pltpu.make_async_copy(dvalues, dvalues_out, pair_sem.at[1])
    values_copy.start()

    @pl.loop(0, count)
    def _(t):
        leaving(t).wait()

    finish(out_copies + [values_copy])


def gradient_kernel(
    scale,
    bounds, g_cols, delta, query, pairs, probs,
    dquery, dkeys_out,
    q_rows, dkeys, weights, dscores, dq_t, in_sem, pair_sem, prob_sem, out_sem,
):
    rows, width = q_rows.shape
    chunks = [slice(r, r + LANES) for r in range(0, rows, LANES)]
    base, count = bounds[0], bounds[1]

    def arriving(t):
        return pltpu.make_async_copy(probs.at[kept_at(t)], weights.at[kept_at(t)], prob_sem.at[t])


    @pl.loop(0, count)
    def _(t):
        arriving(t).start()

    query_copies = head_copies(query, q_rows, in_sem, True)
    begin(query_copies)
    dq_t[...] = jnp.zeros(dq_t.shape, F32)
    dkeys[...] = jnp.zeros(dkeys.shape, BF16)
    finish(query_copies)

    @pl.loop(0, count)
    def _(t):
        at = pl.ds(pl.multiple_of(base + t * TILE, 32), TILE)
        kept = kept_at(t)
        arriving(t).wait()
        value = pairs[at, width : 2 * width]
        for c in chunks:
            dp = dot(value, g_cols[:, c], 1, 0)
            dscores[:, c] = weights[kept, c] * (dp - delta[0:1, c]).astype(BF16)
        dk = dot(dscores[...], q_rows[...], 1, 0)
        dkeys[at, :] = (dk * scale).astype(BF16)
        dq_t[...] += dot(pairs[at, 0:width].T, dscores[...], 1, 0)

    leaving = [pltpu.make_async_copy(dkeys, dkeys_out, pair_sem.at[1])]
    begin(leaving)
    for r in range(0, rows, 128):
        q_rows[r : r + 128, :] = (dq_t[:, r : r + 128].T * scale).astype(BF16)
    out_copies = head_copies(dquery, q_rows, out_sem, False)
    begin(out_copies)
    finish(leaving + out_copies)


VMEM = pl.BlockSpec(memory_space=pltpu.VMEM)
SMEM = pl.BlockSpec(memory_space=pltpu.SMEM)
HBM = pl.BlockSpec(memory_space=pl.ANY)


def call(kernel, name, products, sizes, in_specs, outs, scratch):
    rows, keys, width = sizes
    return pl.pallas_call(
        kernel,
        out_shape=tuple(jax.ShapeDtypeStruct(shape, dtype) for shape, dtype, _ in outs),
        in_specs=in_specs,
        out_specs=tuple(spec for _, _, spec in outs),
        scratch_shapes=scratch,
        compiler_params=pltpu.CompilerParams(vmem_limit_bytes=46 * 1024 * 1024),
        cost_estimate=pl.CostEstimate(
            flops=products * 3 * rows * keys * width, bytes_accessed=20 << 20, transcendentals=0
        ),
        name=name,
    )


def local(device, docs, query, grad, gathered, exchange):
    span, features = query.shape
    keys, width = gathered.shape[0], gathered.shape[1] // 2
    heads = features // width
    rows, most = heads * span, keys // TILE
    sizes = (rows, keys, width)
    scale = 1.0 / math.sqrt(width)
    dma = pltpu.SemaphoreType.DMA
    out, probs, g_cols, delta, bounds, dvalues = call(
        functools.partial(forward_kernel, span, scale), "forward", 3, sizes,
        [SMEM, VMEM, HBM, HBM, VMEM],
        [
            ((span, features), BF16, HBM), ((keys, rows), BF16, HBM), ((width, rows), BF16, VMEM),
            ((8, rows), F32, VMEM), ((2,), I32, SMEM), ((keys, width), BF16, HBM),
        ],
        [
            pltpu.VMEM((rows, width), BF16), pltpu.VMEM((rows, width), BF16),
            pltpu.VMEM((rows, width), BF16),
            pltpu.VMEM((keys, width), BF16), pltpu.VMEM((keys, rows), F32),
            pltpu.VMEM((keys, rows), BF16), pltpu.VMEM((width, rows), F32),
            pltpu.VMEM((8, rows), F32), pltpu.VMEM((8, rows), F32), pltpu.VMEM((8, rows), I32),
            dma((2, heads)), dma((2,)), dma((most,)), dma((heads,)),
        ],
    )(device, docs, query, grad, gathered)
    dvalue_terms = exchange(dvalues)
    dquery, dkeys = call(
        functools.partial(gradient_kernel, scale), "gradient", 3, sizes,
        [SMEM, VMEM, VMEM, HBM, VMEM, HBM],
        [((span, features), BF16, HBM), ((keys, width), BF16, HBM)],
        [
            pltpu.VMEM((rows, width), BF16),
            pltpu.VMEM((keys, width), BF16), pltpu.VMEM((keys, rows), BF16),
            pltpu.VMEM((TILE, rows), BF16), pltpu.VMEM((width, rows), F32),
            dma((heads,)), dma((2,)), dma((most,)), dma((heads,)),
        ],
    )(bounds, g_cols, delta, query, gathered, probs)
    return out, dquery, dkeys, dvalue_terms


def across(blocks, matching, dp_size):
    def turn(mask):
        moves = [(i, i ^ mask) for i in range(dp_size)]
        return lambda *each: tuple(lax.ppermute(v, "dp", moves) for v in each)

    return lax.switch(matching[0] - 1, [turn(mask) for mask in range(1, dp_size)], *blocks)


def on_device(query_rows, key_rows, value_rows, out_grad, doc_ids, matching):
    ctx_size, dp_size = lax.axis_size("ctx"), lax.axis_size("dp")
    me = lax.axis_index("ctx")
    span, width = key_rows.shape[1:]
    end = ctx_size - 1
    is_last = me == end

    def exchange(terms):
        return lax.all_to_all(terms.reshape(ctx_size, span, width), "ctx", 0, 0)

    stored = jnp.concatenate([key_rows[0], value_rows[0]], axis=1)
    arrived, far_docs = across((stored, doc_ids), matching, dp_size)
    docs = jnp.where(is_last, far_docs, doc_ids)
    to_last = (lax.broadcasted_iota(I32, (ctx_size, 1, 1), 0) == end) & jnp.logical_not(is_last)
    gathered = lax.all_to_all(jnp.where(to_last, arrived[None], stored[None]), "ctx", 0, 0)
    out, dquery, dkeys, dvalue_terms = local(
        me.astype(I32)[None], docs, query_rows[0], out_grad[0],
        gathered.reshape(ctx_size * span, 2 * width), exchange,
    )
    both = (exchange(dkeys), dvalue_terms)
    back = across([terms[end] for terms in both], matching, dp_size)

    def final(terms, far):
        own = jnp.sum(terms[:end].astype(F32), axis=0) + far.astype(F32)
        return jnp.where(is_last, terms[end].astype(F32), own).astype(BF16)[None]

    return out[None], dquery[None], final(both[0], back[0]), final(both[1], back[1])


def solution(mesh):
    rows = P("dp", "ctx", None)
    return jax.shard_map(
        on_device,
        mesh=mesh,
        in_specs=(rows, rows, rows, rows, P("dp", None), P()),
        out_specs=(rows, rows, rows, rows),
        check_vma=False,
    )
```

```python
import functools
import math

import jax
import jax.numpy as jnp
from jax import lax
from jax.experimental import pallas as pl
from jax.experimental.pallas import tpu as pltpu
from jax.sharding import PartitionSpec as P

TILE = 512
LANES = 256
BF16, F32, I32 = jnp.bfloat16, jnp.float32, jnp.int32


def dot(a, b, ca, cb):
    return lax.dot_general(a, b, (((ca,), (cb,)), ((), ())), preferred_element_type=F32)


def head_copies(wide, stacked, sem, to_stacked):
    span, width = wide.shape[0], stacked.shape[1]
    made = []
    for h in range(wide.shape[1] // width):
        a = wide.at[:, h * width : (h + 1) * width]
        b = stacked.at[h * span : (h + 1) * span, :]
        a, b = (a, b) if to_stacked else (b, a)
        made.append(pltpu.make_async_copy(a, b, sem.at[h]))
    return made


def begin(copies):
    for c in copies:
        c.start()


def finish(copies):
    for c in copies:
        c.wait()


def kept_at(t):
    return pl.ds(pl.multiple_of(t * TILE, TILE), TILE)


def forward_kernel(
    span, scale,
    device, docs, query, grad, pairs,
    out, probs, g_cols, delta, bounds, dvalues_out,
    q_rows, g_rows, o_rows, dvalues, scores, weights, out_t, top, total, low,
    in_sem, pair_sem, prob_sem, out_sem,
):
    rows, width = q_rows.shape
    key_count = pairs.shape[0]
    heads = rows // span
    chunks = [slice(r, r + LANES) for r in range(0, rows, LANES)]
    factor = scale * math.log2(math.e)
    offset = device[0] * span

    arriving = head_copies(query, q_rows, in_sem.at[0], True)
    grad_copies = head_copies(grad, g_rows, in_sem.at[1], True)
    begin(arriving + grad_copies)

    names = docs[...]
    row = pltpu.roll(names, lax.rem(key_count - offset, key_count), 1)[:, 0:span]
    start = jnp.zeros((1, span), I32)
    for d in range(1, 8):
        before = jnp.sum((names < d).astype(I32), axis=1, keepdims=True)
        start = jnp.where(row == d, before, start)
    place = offset + lax.broadcasted_iota(I32, (1, span), 1)
    for h in range(heads):
        low[0:1, h * span : (h + 1) * span] = start
        low[1:2, h * span : (h + 1) * span] = place
    low_first, low_last = jnp.min(start), jnp.max(start)
    end = offset + span
    count = lax.div(end - low_first + TILE - 1, TILE)
    base = jnp.maximum(end - count * TILE, 0)
    clear = jnp.minimum(lax.div(jnp.maximum(low_last - base, 0) + TILE - 1, TILE), count)
    full = jnp.minimum(jnp.maximum(lax.div(offset + 1 - base, TILE), clear), count)
    bounds[0] = base
    bounds[1] = count

    top[...] = jnp.full(top.shape, -jnp.inf, F32)
    total[...] = jnp.zeros(total.shape, F32)
    out_t[...] = jnp.zeros(out_t.shape, F32)
    dvalues[...] = jnp.zeros(dvalues.shape, BF16)
    finish(arriving)

    def keys_at(t):
        return pl.ds(pl.multiple_of(base + t * TILE, 32), TILE)

    def score_tile(t, masked):
        key = pairs[keys_at(t), 0:width]
        for c in chunks:
            s = dot(key, q_rows[c, :], 1, 1)
            if masked:
                at = base + t * TILE + lax.broadcasted_iota(I32, (TILE, LANES), 0)
                ok = (at >= low[0:1, c]) & (at <= low[1:2, c])
                s = jnp.where(ok, s, -jnp.inf)
            scores[kept_at(t), c] = s
            top[:, c] = jnp.maximum(top[:, c], jnp.max(s.reshape(TILE // 8, 8, LANES), axis=0))

    @pl.loop(0, clear)
    def _(t):
        score_tile(t, True)

    @pl.loop(clear, full)
    def _(t):
        score_tile(t, False)

    @pl.loop(full, count)
    def _(t):
        score_tile(t, True)

    peak = jnp.max(top[...], axis=0, keepdims=True) * factor
    top[...] = jnp.broadcast_to(peak, top.shape)

    def leaving(t):
        return pltpu.make_async_copy(weights.at[kept_at(t)], probs.at[kept_at(t)], prob_sem.at[t])

    @pl.loop(0, count)
    def _(t):
        value_t = pairs[keys_at(t), width : 2 * width].T
        for c in chunks:
            p = jnp.exp2(scores[kept_at(t), c] * factor - top[0:1, c])
            total[:, c] += jnp.sum(p.reshape(TILE // 8, 8, LANES), axis=0)
            weights[kept_at(t), c] = p.astype(BF16)
        leaving(t).start()
        out_t[...] += dot(value_t, weights[kept_at(t), :], 1, 0)

    finish(grad_copies)
    inverse = 1.0 / jnp.sum(total[...], axis=0, keepdims=True)
    for r in range(0, rows, 128):
        c = slice(r, r + 128)
        o = out_t[:, c] * inverse[:, c]
        g = (g_rows[c, :].T.astype(F32) * inverse[:, c]).astype(BF16)
        g_cols[:, c] = g
        delta[0:1, c] = jnp.sum(g.astype(F32) * o, axis=0, keepdims=True)
        o_rows[c, :] = o.T.astype(BF16)
    out_copies = head_copies(out, o_rows, out_sem, False)
    begin(out_copies)

    @pl.loop(0, count)
    def _(t):
        dvalues[keys_at(t), :] = dot(weights[kept_at(t), :], g_cols[...], 1, 1).astype(BF16)

    values_copy = pltpu.make_async_copy(dvalues, dvalues_out, pair_sem.at[1])
    values_copy.start()

    @pl.loop(0, count)
    def _(t):
        leaving(t).wait()

    finish(out_copies + [values_copy])


def gradient_kernel(
    scale,
    bounds, g_cols, delta, query, pairs, probs,
    dquery, dkeys_out,
    q_rows, dkeys, weights, dscores, dq_t, in_sem, pair_sem, prob_sem, out_sem,
):
    rows, width = q_rows.shape
    chunks = [slice(r, r + LANES) for r in range(0, rows, LANES)]
    base, count = bounds[0], bounds[1]

    def arriving(t):
        return pltpu.make_async_copy(probs.at[kept_at(t)], weights.at[kept_at(t)], prob_sem.at[t])


    @pl.loop(0, count)
    def _(t):
        arriving(t).start()

    query_copies = head_copies(query, q_rows, in_sem, True)
    begin(query_copies)
    dq_t[...] = jnp.zeros(dq_t.shape, F32)
    dkeys[...] = jnp.zeros(dkeys.shape, BF16)
    finish(query_copies)

    @pl.loop(0, count)
    def _(t):
        at = pl.ds(pl.multiple_of(base + t * TILE, 32), TILE)
        kept = kept_at(t)
        arriving(t).wait()
        value = pairs[at, width : 2 * width]
        for c in chunks:
            dp = dot(value, g_cols[:, c], 1, 0)
            dscores[:, c] = weights[kept, c] * (dp - delta[0:1, c]).astype(BF16)
        dk = dot(dscores[...], q_rows[...], 1, 0)
        dkeys[at, :] = (dk * scale).astype(BF16)
        dq_t[...] += dot(pairs[at, 0:width].T, dscores[...], 1, 0)

    leaving = [pltpu.make_async_copy(dkeys, dkeys_out, pair_sem.at[1])]
    begin(leaving)
    for r in range(0, rows, 128):
        q_rows[r : r + 128, :] = (dq_t[:, r : r + 128].T * scale).astype(BF16)
    out_copies = head_copies(dquery, q_rows, out_sem, False)
    begin(out_copies)
    finish(leaving + out_copies)


VMEM = pl.BlockSpec(memory_space=pltpu.VMEM)
SMEM = pl.BlockSpec(memory_space=pltpu.SMEM)
HBM = pl.BlockSpec(memory_space=pl.ANY)


def call(kernel, name, products, sizes, in_specs, outs, scratch):
    rows, keys, width = sizes
    return pl.pallas_call(
        kernel,
        out_shape=tuple(jax.ShapeDtypeStruct(shape, dtype) for shape, dtype, _ in outs),
        in_specs=in_specs,
        out_specs=tuple(spec for _, _, spec in outs),
        scratch_shapes=scratch,
        compiler_params=pltpu.CompilerParams(vmem_limit_bytes=46 * 1024 * 1024),
        cost_estimate=pl.CostEstimate(
            flops=products * 3 * rows * keys * width, bytes_accessed=20 << 20, transcendentals=0
        ),
        name=name,
    )


def local(device, docs, query, grad, gathered, exchange):
    span, features = query.shape
    keys, width = gathered.shape[0], gathered.shape[1] // 2
    heads = features // width
    rows, most = heads * span, keys // TILE
    sizes = (rows, keys, width)
    scale = 1.0 / math.sqrt(width)
    dma = pltpu.SemaphoreType.DMA
    out, probs, g_cols, delta, bounds, dvalues = call(
        functools.partial(forward_kernel, span, scale), "forward", 3, sizes,
        [SMEM, VMEM, HBM, HBM, VMEM],
        [
            ((span, features), BF16, HBM), ((keys, rows), BF16, HBM), ((width, rows), BF16, VMEM),
            ((8, rows), F32, VMEM), ((2,), I32, SMEM), ((keys, width), BF16, HBM),
        ],
        [
            pltpu.VMEM((rows, width), BF16), pltpu.VMEM((rows, width), BF16),
            pltpu.VMEM((rows, width), BF16),
            pltpu.VMEM((keys, width), BF16), pltpu.VMEM((keys, rows), F32),
            pltpu.VMEM((keys, rows), BF16), pltpu.VMEM((width, rows), F32),
            pltpu.VMEM((8, rows), F32), pltpu.VMEM((8, rows), F32), pltpu.VMEM((8, rows), I32),
            dma((2, heads)), dma((2,)), dma((most,)), dma((heads,)),
        ],
    )(device, docs, query, grad, gathered)
    dvalue_terms = exchange(dvalues)
    dquery, dkeys = call(
        functools.partial(gradient_kernel, scale), "gradient", 3, sizes,
        [SMEM, VMEM, VMEM, HBM, VMEM, HBM],
        [((span, features), BF16, HBM), ((keys, width), BF16, HBM)],
        [
            pltpu.VMEM((rows, width), BF16),
            pltpu.VMEM((keys, width), BF16), pltpu.VMEM((keys, rows), BF16),
            pltpu.VMEM((TILE, rows), BF16), pltpu.VMEM((width, rows), F32),
            dma((heads,)), dma((2,)), dma((most,)), dma((heads,)),
        ],
    )(bounds, g_cols, delta, query, gathered, probs)
    return out, dquery, dkeys, dvalue_terms


def across(block, matching, dp_size):
    def turn(mask):
        return lambda v: lax.ppermute(v, "dp", [(i, i ^ mask) for i in range(dp_size)])

    return lax.switch(matching[0] - 1, [turn(mask) for mask in range(1, dp_size)], block)


def on_device(query_rows, key_rows, value_rows, out_grad, doc_ids, matching):
    ctx_size, dp_size = lax.axis_size("ctx"), lax.axis_size("dp")
    me = lax.axis_index("ctx")
    span, width = key_rows.shape[1:]
    end = ctx_size - 1
    is_last = me == end

    def exchange(terms):
        return lax.all_to_all(terms.reshape(ctx_size, span, width), "ctx", 0, 0)

    stored = jnp.concatenate([key_rows[0], value_rows[0]], axis=1)
    names = doc_ids.astype(BF16).reshape(-1, 2 * width)
    doc_rows = names.shape[0]
    names = jnp.pad(names, ((0, -doc_rows % 16), (0, 0)))
    arrived = across(jnp.concatenate([stored, names], axis=0), matching, dp_size)
    far_docs = arrived[span : span + doc_rows].reshape(1, -1).astype(I32)
    docs = jnp.where(is_last, far_docs, doc_ids)
    to_last = (lax.broadcasted_iota(I32, (ctx_size, 1, 1), 0) == end) & jnp.logical_not(is_last)
    gathered = lax.all_to_all(jnp.where(to_last, arrived[None, :span], stored[None]), "ctx", 0, 0)
    out, dquery, dkeys, dvalue_terms = local(
        me.astype(I32)[None], docs, query_rows[0], out_grad[0],
        gathered.reshape(ctx_size * span, 2 * width), exchange,
    )
    both = (exchange(dkeys), dvalue_terms)
    tail = jnp.concatenate([terms[end] for terms in both], axis=1)
    back = across(tail, matching, dp_size)

    def final(terms, far):
        own = jnp.sum(terms[:end].astype(F32), axis=0) + far.astype(F32)
        return jnp.where(is_last, terms[end].astype(F32), own).astype(BF16)[None]

    return out[None], dquery[None], final(both[0], back[:, :width]), final(both[1], back[:, width:])


def solution(mesh):
    rows = P("dp", "ctx", None)
    return jax.shard_map(
        on_device,
        mesh=mesh,
        in_specs=(rows, rows, rows, rows, P("dp", None), P()),
        out_specs=(rows, rows, rows, rows),
        check_vma=False,
    )
```

```python
import functools
import math

import jax
import jax.numpy as jnp
from jax import lax
from jax.experimental import pallas as pl
from jax.experimental.pallas import tpu as pltpu
from jax.sharding import PartitionSpec as P

TILE = 768
LONGEST = 2688
LANES = 256
BF16, F32, I32 = jnp.bfloat16, jnp.float32, jnp.int32


def dot(a, b, ca, cb):
    return lax.dot_general(a, b, (((ca,), (cb,)), ((), ())), preferred_element_type=F32)


def head_copies(wide, stacked, sem, to_stacked):
    span, width = wide.shape[0], stacked.shape[1]
    made = []
    for h in range(wide.shape[1] // width):
        a = wide.at[:, h * width : (h + 1) * width]
        b = stacked.at[h * span : (h + 1) * span, :]
        a, b = (a, b) if to_stacked else (b, a)
        made.append(pltpu.make_async_copy(a, b, sem.at[h]))
    return made


def begin(copies):
    for c in copies:
        c.start()


def finish(copies):
    for c in copies:
        c.wait()


def kept_at(t):
    return pl.ds(pl.multiple_of(t * TILE, TILE), TILE)


def attention_kernel(
    span, scale,
    device, docs, query, grad, pairs,
    out, dquery, terms,
    q_rows, g_rows, o_rows, g_cols, dkeys, dvalues, scores, weights, dscores, out_t, dq_t, top, total, low,
    in_sem, pair_sem, out_sem,
):
    rows, width = q_rows.shape
    key_count = pairs.shape[0]
    heads = rows // span
    chunks = [slice(r, r + LANES) for r in range(0, rows, LANES)]
    factor = scale * math.log2(math.e)
    offset = device[0] * span

    arriving = head_copies(query, q_rows, in_sem.at[0], True)
    grad_copies = head_copies(grad, g_rows, in_sem.at[1], True)
    begin(arriving + grad_copies)

    names = docs[...]
    row = pltpu.roll(names, lax.rem(key_count - offset, key_count), 1)[:, 0:span]
    start = jnp.zeros((1, span), I32)
    for d in range(1, 8):
        before = jnp.sum((names < d).astype(I32), axis=1, keepdims=True)
        start = jnp.where(row == d, before, start)
    place = offset + lax.broadcasted_iota(I32, (1, span), 1)
    for h in range(heads):
        low[0:1, h * span : (h + 1) * span] = start
        low[1:2, h * span : (h + 1) * span] = place
    low_first, low_last = jnp.min(start), jnp.max(start)
    end = offset + span
    count = lax.div(end - low_first + TILE - 1, TILE)
    base = jnp.maximum(end - count * TILE, 0)
    clear = jnp.minimum(lax.div(jnp.maximum(low_last - base, 0) + TILE - 1, TILE), count)
    full = jnp.minimum(jnp.maximum(lax.div(offset + 1 - base, TILE), clear), count)

    top[...] = jnp.full(top.shape, -jnp.inf, F32)
    total[...] = jnp.zeros(total.shape, F32)
    out_t[...] = jnp.zeros(out_t.shape, F32)
    dq_t[...] = jnp.zeros(dq_t.shape, F32)
    dvalues[...] = jnp.zeros(dvalues.shape, BF16)
    dkeys[...] = jnp.zeros(dkeys.shape, BF16)
    finish(arriving)

    def keys_at(t):
        return pl.ds(pl.multiple_of(base + t * TILE, 32), TILE)

    def score_tile(t, masked):
        key = pairs[keys_at(t), 0:width]
        for c in chunks:
            s = dot(key, q_rows[c, :], 1, 1)
            if masked:
                at = base + t * TILE + lax.broadcasted_iota(I32, (TILE, LANES), 0)
                ok = (at >= low[0:1, c]) & (at <= low[1:2, c])
                s = jnp.where(ok, s, -jnp.inf)
            scores[kept_at(t), c] = s
            top[:, c] = jnp.maximum(top[:, c], jnp.max(s.reshape(TILE // 8, 8, LANES), axis=0))

    @pl.loop(0, clear)
    def _(t):
        score_tile(t, True)

    @pl.loop(clear, full)
    def _(t):
        score_tile(t, False)

    @pl.loop(full, count)
    def _(t):
        score_tile(t, True)

    peak = jnp.max(top[...], axis=0, keepdims=True) * factor
    top[...] = jnp.broadcast_to(peak, top.shape)

    @pl.loop(0, count)
    def _(t):
        value_t = pairs[keys_at(t), width : 2 * width].T
        for c in chunks:
            p = jnp.exp2(scores[kept_at(t), c] * factor - top[0:1, c])
            total[:, c] += jnp.sum(p.reshape(TILE // 8, 8, LANES), axis=0)
            weights[kept_at(t), c] = p.astype(BF16)
        out_t[...] += dot(value_t, weights[kept_at(t), :], 1, 0)

    finish(grad_copies)
    inverse = 1.0 / jnp.sum(total[...], axis=0, keepdims=True)
    for r in range(0, rows, 128):
        c = slice(r, r + 128)
        o = out_t[:, c] * inverse[:, c]
        g = (g_rows[c, :].T.astype(F32) * inverse[:, c]).astype(BF16)
        g_cols[:, c] = g
        top[0:1, c] = jnp.sum(g.astype(F32) * o, axis=0, keepdims=True)
        o_rows[c, :] = o.T.astype(BF16)
    out_copies = head_copies(out, o_rows, out_sem.at[0], False)
    begin(out_copies)

    @pl.loop(0, count)
    def _(t):
        dvalues[keys_at(t), :] = dot(weights[kept_at(t), :], g_cols[...], 1, 1).astype(BF16)

    values_copy = pltpu.make_async_copy(dvalues, terms.at[:, width : 2 * width], pair_sem.at[1])
    values_copy.start()

    @pl.loop(0, count)
    def _(t):
        at, kept = keys_at(t), kept_at(t)
        value = pairs[at, width : 2 * width]
        for c in chunks:
            dp = dot(value, g_cols[:, c], 1, 0)
            dscores[:, c] = weights[kept, c] * (dp - top[0:1, c]).astype(BF16)
        dk = dot(dscores[...], q_rows[...], 1, 0)
        dkeys[at, :] = (dk * scale).astype(BF16)
        dq_t[...] += dot(pairs[at, 0:width].T, dscores[...], 1, 0)

    keys_copy = pltpu.make_async_copy(dkeys, terms.at[:, 0:width], pair_sem.at[0])
    keys_copy.start()
    for r in range(0, rows, 128):
        g_rows[r : r + 128, :] = (dq_t[:, r : r + 128].T * scale).astype(BF16)
    last_copies = head_copies(dquery, g_rows, out_sem.at[1], False)
    begin(last_copies)
    finish(out_copies + [values_copy, keys_copy] + last_copies)


VMEM = pl.BlockSpec(memory_space=pltpu.VMEM)
SMEM = pl.BlockSpec(memory_space=pltpu.SMEM)
HBM = pl.BlockSpec(memory_space=pl.ANY)


def attention(device, docs, query, grad, gathered):
    span, features = query.shape
    keys, width = gathered.shape[0], gathered.shape[1] // 2
    heads = features // width
    rows = heads * span
    kept = (span + LONGEST - 1 + TILE - 1) // TILE * TILE
    dma = pltpu.SemaphoreType.DMA
    return pl.pallas_call(
        functools.partial(attention_kernel, span, 1.0 / math.sqrt(width)),
        out_shape=(
            jax.ShapeDtypeStruct((span, features), BF16),
            jax.ShapeDtypeStruct((span, features), BF16),
            jax.ShapeDtypeStruct((keys, 2 * width), BF16),
        ),
        in_specs=[SMEM, VMEM, HBM, HBM, VMEM],
        out_specs=(HBM, HBM, HBM),
        scratch_shapes=[
            pltpu.VMEM((rows, width), BF16), pltpu.VMEM((rows, width), BF16),
            pltpu.VMEM((rows, width), BF16), pltpu.VMEM((width, rows), BF16),
            pltpu.VMEM((keys, width), BF16), pltpu.VMEM((keys, width), BF16),
            pltpu.VMEM((kept, rows), F32), pltpu.VMEM((kept, rows), BF16),
            pltpu.VMEM((TILE, rows), BF16),
            pltpu.VMEM((width, rows), F32), pltpu.VMEM((width, rows), F32),
            pltpu.VMEM((8, rows), F32), pltpu.VMEM((8, rows), F32), pltpu.VMEM((8, rows), I32),
            dma((2, heads)), dma((2,)), dma((2, heads)),
        ],
        compiler_params=pltpu.CompilerParams(vmem_limit_bytes=46 << 20),
        cost_estimate=pl.CostEstimate(
            flops=12 * rows * keys * width // 2, bytes_accessed=6 << 20, transcendentals=rows * keys // 2
        ),
        name="attention",
    )(device, docs, query, grad, gathered)


def across(block, matching, dp_size):
    def turn(mask):
        return lambda v: lax.ppermute(v, "dp", [(i, i ^ mask) for i in range(dp_size)])

    return lax.switch(matching[0] - 1, [turn(mask) for mask in range(1, dp_size)], block)


def on_device(query_rows, key_rows, value_rows, out_grad, doc_ids, matching):
    ctx_size, dp_size = lax.axis_size("ctx"), lax.axis_size("dp")
    me = lax.axis_index("ctx")
    span, width = key_rows.shape[1:]
    end = ctx_size - 1
    is_last = me == end

    stored = jnp.concatenate([key_rows[0], value_rows[0]], axis=1)
    names = doc_ids.astype(BF16).reshape(-1, 2 * width)
    doc_rows = names.shape[0]
    names = jnp.pad(names, ((0, -doc_rows % 16), (0, 0)))
    arrived = across(jnp.concatenate([stored, names], axis=0), matching, dp_size)
    far_docs = arrived[span : span + doc_rows].reshape(1, -1).astype(I32)
    docs = jnp.where(is_last, far_docs, doc_ids)
    to_last = (lax.broadcasted_iota(I32, (ctx_size, 1, 1), 0) == end) & jnp.logical_not(is_last)
    gathered = lax.all_to_all(jnp.where(to_last, arrived[None, :span], stored[None]), "ctx", 0, 0)
    out, dquery, terms = attention(
        me.astype(I32)[None], docs, query_rows[0], out_grad[0],
        gathered.reshape(ctx_size * span, 2 * width),
    )
    terms = lax.all_to_all(terms.reshape(ctx_size, span, 2 * width), "ctx", 0, 0)
    tail = terms[end]
    own = jnp.sum(terms[:end].astype(F32), axis=0)
    back = across(tail, matching, dp_size)
    final = jnp.where(is_last, tail.astype(F32), own + back.astype(F32)).astype(BF16)
    return out[None], dquery[None], final[None, :, :width], final[None, :, width:]


def solution(mesh):
    rows = P("dp", "ctx", None)
    return jax.shard_map(
        on_device,
        mesh=mesh,
        in_specs=(rows, rows, rows, rows, P("dp", None), P()),
        out_specs=(rows, rows, rows, rows),
        check_vma=False,
    )
```

```python
import functools
import math

import jax
import jax.numpy as jnp
from jax import lax
from jax.experimental import pallas as pl
from jax.experimental.pallas import tpu as pltpu
from jax.sharding import PartitionSpec as P

TILE = 736
LONGEST = 2688
LANES = 1792
BF16, F32, I32 = jnp.bfloat16, jnp.float32, jnp.int32


def dot(a, b, ca, cb):
    return lax.dot_general(a, b, (((ca,), (cb,)), ((), ())), preferred_element_type=F32)


def head_copies(wide, stacked, sem, to_stacked):
    span, width = wide.shape[0], stacked.shape[1]
    made = []
    for h in range(wide.shape[1] // width):
        a = wide.at[:, h * width : (h + 1) * width]
        b = stacked.at[h * span : (h + 1) * span, :]
        a, b = (a, b) if to_stacked else (b, a)
        made.append(pltpu.make_async_copy(a, b, sem.at[h]))
    return made


def begin(copies):
    for c in copies:
        c.start()


def finish(copies):
    for c in copies:
        c.wait()


def kept_at(t):
    return pl.ds(pl.multiple_of(t * TILE, TILE), TILE)


def attention_kernel(
    span, scale,
    device, docs, query, grad, pairs,
    out, dquery, terms,
    q_rows, g_rows, o_rows, g_cols, dkeys, dvalues, scores, weights, dscores, out_t, dq_t, top, total, low,
    in_sem, pair_sem, out_sem,
):
    rows, width = q_rows.shape
    key_count = pairs.shape[0]
    heads = rows // span
    chunks = [slice(r, r + LANES) for r in range(0, rows, LANES)]
    factor = scale * math.log2(math.e)
    offset = device[0] * span

    arriving = head_copies(query, q_rows, in_sem.at[0], True)
    grad_copies = head_copies(grad, g_rows, in_sem.at[1], True)
    begin(arriving + grad_copies)

    names = docs[...]
    row = pltpu.roll(names, lax.rem(key_count - offset, key_count), 1)[:, 0:span]
    start = jnp.zeros((1, span), I32)
    for d in range(1, 8):
        before = jnp.sum((names < d).astype(I32), axis=1, keepdims=True)
        start = jnp.where(row == d, before, start)
    place = offset + lax.broadcasted_iota(I32, (1, span), 1)
    for h in range(heads):
        low[0:1, h * span : (h + 1) * span] = start
        low[1:2, h * span : (h + 1) * span] = place
    low_first, low_last = jnp.min(start), jnp.max(start)
    end = offset + span
    count = lax.div(end - low_first + TILE - 1, TILE)
    base = jnp.maximum(end - count * TILE, 0)
    clear = jnp.minimum(lax.div(jnp.maximum(low_last - base, 0) + TILE - 1, TILE), count)
    full = jnp.minimum(jnp.maximum(lax.div(offset + 1 - base, TILE), clear), count)

    top[...] = jnp.full(top.shape, -jnp.inf, F32)
    total[...] = jnp.zeros(total.shape, F32)
    out_t[...] = jnp.zeros(out_t.shape, F32)
    dq_t[...] = jnp.zeros(dq_t.shape, F32)
    dvalues[...] = jnp.zeros(dvalues.shape, BF16)
    dkeys[...] = jnp.zeros(dkeys.shape, BF16)
    finish(arriving)

    def keys_at(t):
        return pl.ds(pl.multiple_of(base + t * TILE, 32), TILE)

    def score_tile(t, masked):
        key = pairs[keys_at(t), 0:width]
        for c in chunks:
            s = dot(key, q_rows[c, :], 1, 1)
            if masked:
                at = base + t * TILE + lax.broadcasted_iota(I32, (TILE, LANES), 0)
                ok = (at >= low[0:1, c]) & (at <= low[1:2, c])
                s = jnp.where(ok, s, -jnp.inf)
            scores[kept_at(t), c] = s
            top[:, c] = jnp.maximum(top[:, c], jnp.max(s.reshape(TILE // 8, 8, LANES), axis=0))

    @pl.loop(0, clear)
    def _(t):
        score_tile(t, True)

    @pl.loop(clear, full)
    def _(t):
        score_tile(t, False)

    @pl.loop(full, count)
    def _(t):
        score_tile(t, True)

    peak = jnp.max(top[...], axis=0, keepdims=True) * factor
    top[...] = jnp.broadcast_to(peak, top.shape)

    @pl.loop(0, count)
    def _(t):
        value_t = pairs[keys_at(t), width : 2 * width].T
        for c in chunks:
            p = jnp.exp2(scores[kept_at(t), c] * factor - top[0:1, c])
            total[:, c] += jnp.sum(p.reshape(TILE // 8, 8, LANES), axis=0)
            weights[kept_at(t), c] = p.astype(BF16)
        out_t[...] += dot(value_t, weights[kept_at(t), :], 1, 0)

    finish(grad_copies)
    inverse = 1.0 / jnp.sum(total[...], axis=0, keepdims=True)
    for r in range(0, rows, 128):
        c = slice(r, r + 128)
        o = out_t[:, c] * inverse[:, c]
        g = (g_rows[c, :].T.astype(F32) * inverse[:, c]).astype(BF16)
        g_cols[:, c] = g
        top[0:1, c] = jnp.sum(g.astype(F32) * o, axis=0, keepdims=True)
        o_rows[c, :] = o.T.astype(BF16)
    out_copies = head_copies(out, o_rows, out_sem.at[0], False)
    begin(out_copies)

    @pl.loop(0, count)
    def _(t):
        dvalues[keys_at(t), :] = dot(weights[kept_at(t), :], g_cols[...], 1, 1).astype(BF16)

    values_copy = pltpu.make_async_copy(dvalues, terms.at[:, width : 2 * width], pair_sem.at[1])
    values_copy.start()

    @pl.loop(0, count)
    def _(t):
        at, kept = keys_at(t), kept_at(t)
        value = pairs[at, width : 2 * width]
        for c in chunks:
            dp = dot(value, g_cols[:, c], 1, 0)
            dscores[:, c] = weights[kept, c] * (dp - top[0:1, c]).astype(BF16)
        dk = dot(dscores[...], q_rows[...], 1, 0)
        dkeys[at, :] = (dk * scale).astype(BF16)
        dq_t[...] += dot(pairs[at, 0:width].T, dscores[...], 1, 0)

    keys_copy = pltpu.make_async_copy(dkeys, terms.at[:, 0:width], pair_sem.at[0])
    keys_copy.start()
    for r in range(0, rows, 128):
        g_rows[r : r + 128, :] = (dq_t[:, r : r + 128].T * scale).astype(BF16)
    last_copies = head_copies(dquery, g_rows, out_sem.at[1], False)
    begin(last_copies)
    finish(out_copies + [values_copy, keys_copy] + last_copies)


VMEM = pl.BlockSpec(memory_space=pltpu.VMEM)
SMEM = pl.BlockSpec(memory_space=pltpu.SMEM)
HBM = pl.BlockSpec(memory_space=pl.ANY)


def attention(device, docs, query, grad, gathered):
    span, features = query.shape
    keys, width = gathered.shape[0], gathered.shape[1] // 2
    heads = features // width
    rows = heads * span
    kept = (span + LONGEST - 1 + TILE - 1) // TILE * TILE
    dma = pltpu.SemaphoreType.DMA
    return pl.pallas_call(
        functools.partial(attention_kernel, span, 1.0 / math.sqrt(width)),
        out_shape=(
            jax.ShapeDtypeStruct((span, features), BF16),
            jax.ShapeDtypeStruct((span, features), BF16),
            jax.ShapeDtypeStruct((keys, 2 * width), BF16),
        ),
        in_specs=[SMEM, VMEM, HBM, HBM, VMEM],
        out_specs=(HBM, HBM, HBM),
        scratch_shapes=[
            pltpu.VMEM((rows, width), BF16), pltpu.VMEM((rows, width), BF16),
            pltpu.VMEM((rows, width), BF16), pltpu.VMEM((width, rows), BF16),
            pltpu.VMEM((keys, width), BF16), pltpu.VMEM((keys, width), BF16),
            pltpu.VMEM((kept, rows), F32), pltpu.VMEM((kept, rows), BF16),
            pltpu.VMEM((TILE, rows), BF16),
            pltpu.VMEM((width, rows), F32), pltpu.VMEM((width, rows), F32),
            pltpu.VMEM((8, rows), F32), pltpu.VMEM((8, rows), F32), pltpu.VMEM((8, rows), I32),
            dma((2, heads)), dma((2,)), dma((2, heads)),
        ],
        compiler_params=pltpu.CompilerParams(vmem_limit_bytes=46 << 20),
        cost_estimate=pl.CostEstimate(
            flops=12 * rows * keys * width // 2, bytes_accessed=6 << 20, transcendentals=rows * keys // 2
        ),
        name="attention",
    )(device, docs, query, grad, gathered)


def across(block, matching, dp_size):
    def turn(mask):
        return lambda v: lax.ppermute(v, "dp", [(i, i ^ mask) for i in range(dp_size)])

    return lax.switch(matching[0] - 1, [turn(mask) for mask in range(1, dp_size)], block)


def on_device(query_rows, key_rows, value_rows, out_grad, doc_ids, matching):
    ctx_size, dp_size = lax.axis_size("ctx"), lax.axis_size("dp")
    me = lax.axis_index("ctx")
    span, width = key_rows.shape[1:]
    end = ctx_size - 1
    is_last = me == end

    stored = jnp.concatenate([key_rows[0], value_rows[0]], axis=1)
    names = doc_ids.astype(BF16).reshape(-1, 2 * width)
    doc_rows = names.shape[0]
    names = jnp.pad(names, ((0, -doc_rows % 16), (0, 0)))
    arrived = across(jnp.concatenate([stored, names], axis=0), matching, dp_size)
    far_docs = arrived[span : span + doc_rows].reshape(1, -1).astype(I32)
    docs = jnp.where(is_last, far_docs, doc_ids)
    to_last = (lax.broadcasted_iota(I32, (ctx_size, 1, 1), 0) == end) & jnp.logical_not(is_last)
    gathered = lax.all_to_all(jnp.where(to_last, arrived[None, :span], stored[None]), "ctx", 0, 0)
    out, dquery, terms = attention(
        me.astype(I32)[None], docs, query_rows[0], out_grad[0],
        gathered.reshape(ctx_size * span, 2 * width),
    )
    terms = lax.all_to_all(terms.reshape(ctx_size, span, 2 * width), "ctx", 0, 0)
    tail = terms[end]
    own = jnp.sum(terms[:end].astype(F32), axis=0)
    back = across(tail, matching, dp_size)
    final = jnp.where(is_last, tail.astype(F32), own + back.astype(F32)).astype(BF16)
    return out[None], dquery[None], final[None, :, :width], final[None, :, width:]


def solution(mesh):
    rows = P("dp", "ctx", None)
    return jax.shard_map(
        on_device,
        mesh=mesh,
        in_specs=(rows, rows, rows, rows, P("dp", None), P()),
        out_specs=(rows, rows, rows, rows),
        check_vma=False,
    )
```

```python
import functools
import math

import jax
import jax.numpy as jnp
from jax import lax
from jax.experimental import pallas as pl
from jax.experimental.pallas import tpu as pltpu
from jax.sharding import PartitionSpec as P

TILE = 736
LONGEST = 2688
LANES = 1792
BF16, F32, I32 = jnp.bfloat16, jnp.float32, jnp.int32


def dot(a, b, ca, cb):
    return lax.dot_general(a, b, (((ca,), (cb,)), ((), ())), preferred_element_type=F32)


def head_copies(wide, stacked, sem, to_stacked):
    span, width = wide.shape[0], stacked.shape[1]
    made = []
    for h in range(wide.shape[1] // width):
        a = wide.at[:, h * width : (h + 1) * width]
        b = stacked.at[h * span : (h + 1) * span, :]
        a, b = (a, b) if to_stacked else (b, a)
        made.append(pltpu.make_async_copy(a, b, sem.at[h]))
    return made


def begin(copies):
    for c in copies:
        c.start()


def finish(copies):
    for c in copies:
        c.wait()


def kept_at(t):
    return pl.ds(pl.multiple_of(t * TILE, TILE), TILE)


def attention_kernel(
    span, scale,
    device, docs, query, grad, pairs,
    out, dquery, terms,
    q_rows, g_rows, o_rows, g_cols, dkeys, dvalues, scores, weights, dscores, out_t, dq_t, top, total, low,
    in_sem, pair_sem, out_sem,
):
    rows, width = q_rows.shape
    key_count = pairs.shape[0]
    heads = rows // span
    chunks = [slice(r, r + LANES) for r in range(0, rows, LANES)]
    factor = scale * math.log2(math.e)
    offset = device[0] * span

    arriving = head_copies(query, q_rows, in_sem.at[0], True)
    grad_copies = head_copies(grad, g_rows, in_sem.at[1], True)
    begin(arriving + grad_copies)

    names = docs[...]
    row = pltpu.roll(names, lax.rem(key_count - offset, key_count), 1)[:, 0:span]
    start = jnp.zeros((1, span), I32)
    for d in range(1, 8):
        before = jnp.sum((names < d).astype(I32), axis=1, keepdims=True)
        start = jnp.where(row == d, before, start)
    place = offset + lax.broadcasted_iota(I32, (1, span), 1)
    for h in range(heads):
        low[0:1, h * span : (h + 1) * span] = start
        low[1:2, h * span : (h + 1) * span] = place
    low_first, low_last = jnp.min(start), jnp.max(start)
    end = offset + span
    count = lax.div(end - low_first + TILE - 1, TILE)
    base = jnp.maximum(end - count * TILE, 0)
    clear = jnp.minimum(lax.div(jnp.maximum(low_last - base, 0) + TILE - 1, TILE), count)
    full = jnp.minimum(jnp.maximum(lax.div(offset + 1 - base, TILE), clear), count)

    top[...] = jnp.full(top.shape, -jnp.inf, F32)
    total[...] = jnp.zeros(total.shape, F32)
    out_t[...] = jnp.zeros(out_t.shape, F32)
    dq_t[...] = jnp.zeros(dq_t.shape, F32)
    dvalues[...] = jnp.zeros(dvalues.shape, BF16)
    dkeys[...] = jnp.zeros(dkeys.shape, BF16)
    finish(arriving)

    def keys_at(t):
        return pl.ds(pl.multiple_of(base + t * TILE, 32), TILE)

    def score_tile(t, masked):
        key = pairs[keys_at(t), 0:width]
        for c in chunks:
            s = dot(key, q_rows[c, :], 1, 1)
            if masked:
                at = base + t * TILE + lax.broadcasted_iota(I32, (TILE, LANES), 0)
                ok = (at >= low[0:1, c]) & (at <= low[1:2, c])
                s = jnp.where(ok, s, -jnp.inf)
            scores[kept_at(t), c] = s
            top[:, c] = jnp.maximum(top[:, c], jnp.max(s.reshape(TILE // 8, 8, LANES), axis=0))

    @pl.loop(0, clear)
    def _(t):
        score_tile(t, True)

    @pl.loop(clear, full)
    def _(t):
        score_tile(t, False)

    @pl.loop(full, count)
    def _(t):
        score_tile(t, True)

    peak = jnp.max(top[...], axis=0, keepdims=True) * factor
    top[...] = jnp.broadcast_to(peak, top.shape)

    @pl.loop(0, count)
    def _(t):
        value_t = pairs[keys_at(t), width : 2 * width].T
        for c in chunks:
            p = jnp.exp2(scores[kept_at(t), c] * factor - top[0:1, c])
            total[:, c] += jnp.sum(p.reshape(TILE // 8, 8, LANES), axis=0)
            weights[kept_at(t), c] = p.astype(BF16)
        out_t[...] += dot(value_t, weights[kept_at(t), :], 1, 0)

    finish(grad_copies)
    inverse = 1.0 / jnp.sum(total[...], axis=0, keepdims=True)
    for r in range(0, rows, 128):
        c = slice(r, r + 128)
        o = out_t[:, c] * inverse[:, c]
        g = (g_rows[c, :].T.astype(F32) * inverse[:, c]).astype(BF16)
        g_cols[:, c] = g
        top[0:1, c] = jnp.sum(g.astype(F32) * o, axis=0, keepdims=True)
        o_rows[c, :] = o.T.astype(BF16)
    out_copies = head_copies(out, o_rows, out_sem.at[0], False)
    begin(out_copies)

    @pl.loop(0, count)
    def _(t):
        dvalues[keys_at(t), :] = dot(weights[kept_at(t), :], g_cols[...], 1, 1).astype(BF16)

    values_copy = pltpu.make_async_copy(dvalues, terms.at[:, width : 2 * width], pair_sem.at[1])
    values_copy.start()

    @pl.loop(0, count)
    def _(t):
        at, kept = keys_at(t), kept_at(t)
        value = pairs[at, width : 2 * width]
        for c in chunks:
            dp = dot(value, g_cols[:, c], 1, 0)
            dscores[:, c] = weights[kept, c] * (dp - top[0:1, c]).astype(BF16)
        dk = dot(dscores[...], q_rows[...], 1, 0)
        dkeys[at, :] = (dk * scale).astype(BF16)
        dq_t[...] += dot(pairs[at, 0:width].T, dscores[...], 1, 0)

    keys_copy = pltpu.make_async_copy(dkeys, terms.at[:, 0:width], pair_sem.at[0])
    keys_copy.start()
    for r in range(0, rows, 128):
        g_rows[r : r + 128, :] = (dq_t[:, r : r + 128].T * scale).astype(BF16)
    last_copies = head_copies(dquery, g_rows, out_sem.at[1], False)
    begin(last_copies)
    finish(out_copies + [values_copy, keys_copy] + last_copies)


VMEM = pl.BlockSpec(memory_space=pltpu.VMEM)
SMEM = pl.BlockSpec(memory_space=pltpu.SMEM)
HBM = pl.BlockSpec(memory_space=pl.ANY)


def attention(device, docs, query, grad, gathered):
    span, features = query.shape
    keys, width = gathered.shape[0], gathered.shape[1] // 2
    heads = features // width
    rows = heads * span
    kept = (span + LONGEST - 1 + TILE - 1) // TILE * TILE
    dma = pltpu.SemaphoreType.DMA
    return pl.pallas_call(
        functools.partial(attention_kernel, span, 1.0 / math.sqrt(width)),
        out_shape=(
            jax.ShapeDtypeStruct((span, features), BF16),
            jax.ShapeDtypeStruct((span, features), BF16),
            jax.ShapeDtypeStruct((keys, 2 * width), BF16),
        ),
        in_specs=[SMEM, VMEM, HBM, HBM, VMEM],
        out_specs=(HBM, HBM, HBM),
        scratch_shapes=[
            pltpu.VMEM((rows, width), BF16), pltpu.VMEM((rows, width), BF16),
            pltpu.VMEM((rows, width), BF16), pltpu.VMEM((width, rows), BF16),
            pltpu.VMEM((keys, width), BF16), pltpu.VMEM((keys, width), BF16),
            pltpu.VMEM((kept, rows), F32), pltpu.VMEM((kept, rows), BF16),
            pltpu.VMEM((TILE, rows), BF16),
            pltpu.VMEM((width, rows), F32), pltpu.VMEM((width, rows), F32),
            pltpu.VMEM((8, rows), F32), pltpu.VMEM((8, rows), F32), pltpu.VMEM((8, rows), I32),
            dma((2, heads)), dma((2,)), dma((2, heads)),
        ],
        compiler_params=pltpu.CompilerParams(vmem_limit_bytes=46 << 20),
        cost_estimate=pl.CostEstimate(
            flops=12 * rows * keys * width // 2, bytes_accessed=6 << 20, transcendentals=rows * keys // 2
        ),
        name="attention",
    )(device, docs, query, grad, gathered)


def spread_kernel(device, mine, far, sending, sems):
    slots, span = sending.shape[0], sending.shape[1]
    last = slots - 1
    copies = [
        pltpu.make_async_copy(mine.at[0:span, :], sending.at[i], sems.at[i]) for i in range(slots)
    ]
    partner = pltpu.make_async_copy(far.at[0:span, :], sending.at[last], sems.at[last])
    begin(copies[:last])

    @pl.when(device[0] == last)
    def _():
        copies[last].start()

    @pl.when(device[0] != last)
    def _():
        partner.start()

    finish(copies)


def spread(device, mine, far, slots, span):
    return pl.pallas_call(
        spread_kernel,
        out_shape=jax.ShapeDtypeStruct((slots, span, mine.shape[1]), mine.dtype),
        in_specs=[SMEM, HBM, HBM],
        out_specs=HBM,
        scratch_shapes=[pltpu.SemaphoreType.DMA((slots,))],
        name="spread",
    )(device, mine, far)


def across(block, matching, dp_size):
    def turn(mask):
        return lambda v: lax.ppermute(v, "dp", [(i, i ^ mask) for i in range(dp_size)])

    return lax.switch(matching[0] - 1, [turn(mask) for mask in range(1, dp_size)], block)


def on_device(query_rows, key_rows, value_rows, out_grad, doc_ids, matching):
    ctx_size, dp_size = lax.axis_size("ctx"), lax.axis_size("dp")
    me = lax.axis_index("ctx")
    span, width = key_rows.shape[1:]
    end = ctx_size - 1
    is_last = me == end

    stored = jnp.concatenate([key_rows[0], value_rows[0]], axis=1)
    names = doc_ids.astype(BF16).reshape(-1, 2 * width)
    doc_rows = names.shape[0]
    names = jnp.pad(names, ((0, -doc_rows % 16), (0, 0)))
    leaving = jnp.concatenate([stored, names], axis=0)
    arrived = across(leaving, matching, dp_size)
    far_docs = arrived[span : span + doc_rows].reshape(1, -1).astype(I32)
    docs = jnp.where(is_last, far_docs, doc_ids)
    device = me.astype(I32)[None]
    sending = spread(device, leaving, arrived, ctx_size, span)
    gathered = lax.all_to_all(sending, "ctx", 0, 0)
    out, dquery, terms = attention(
        device, docs, query_rows[0], out_grad[0],
        gathered.reshape(ctx_size * span, 2 * width),
    )
    terms = lax.all_to_all(terms.reshape(ctx_size, span, 2 * width), "ctx", 0, 0)
    tail = terms[end]
    own = jnp.sum(terms[:end].astype(F32), axis=0)
    back = across(tail, matching, dp_size)
    final = jnp.where(is_last, tail.astype(F32), own + back.astype(F32)).astype(BF16)
    return out[None], dquery[None], final[None, :, :width], final[None, :, width:]


def solution(mesh):
    rows = P("dp", "ctx", None)
    return jax.shard_map(
        on_device,
        mesh=mesh,
        in_specs=(rows, rows, rows, rows, P("dp", None), P()),
        out_specs=(rows, rows, rows, rows),
        check_vma=False,
    )
```
